128 devices in a mesh: row: 16 (over z, x_hi, core), rep: 8 (over y, x_lo).
Axes of the slice: x: 4 (x_hi: 2, x_lo: 2; x = x_hi * 2 + x_lo), y: 4, z: 4, core: 2. Of those that a mesh axis runs over, the one named last changes fastest.
Arguments:
- features: float32 [131072, 128], P(('row', 'rep')), may hold values from -6 to 6
- weight: float32 [128, 128], replicated, may hold values from -0.5 to 0.5
- adjacency_tiles: float32 [40960, 128, 128], P(('row', 'rep')), may hold values from 0 to 0.05
- tile_rows: int32 [40960], P(('row', 'rep')), may hold values from 0 to 63
- tile_cols: int32 [40960], P(('row', 'rep')), may hold values from 0 to 127
- tile_counts: int32 [128], P(('row', 'rep')), may hold values from 1 to 320, as said below
- cluster_order: int32 [128, 1024], P(('row', 'rep')), may hold values from 0 to 1023, each once within a row
Outputs:
- activations: float32 [131072, 128], P(('row', 'rep'))
The draws below stay inside these ranges and needn't reach their ends.
Inputs may be any that keep to these rules, and one draw needn't show every extreme that they name: `tile_counts`: every device has at least one live slot; some device fills all 320.
All inputs are finite; a program needn't handle non-finite values.
Results may differ from the reference program's by a relative error of at most 0.0003.
Values sent between devices are 32-bit elements; how exact they have to be, the bound alone decides.
A program may use at most 128 MiB of HBM per device.

```python
import jax
import jax.numpy as jnp
from jax import lax

FEAT = 128
SLAB = 1024
TILES_DEV = 320
NODES = 131072
TILES = 40960
ROW_TILES = 64
COL_TILES = 128
N_ROW = 16
N_REP = 8


def draw_tile_counts(key, part):
    key = jax.random.fold_in(key, 5)
    first_key, second_key = jax.random.split(key)
    lowest = max(1, TILES_DEV // 4)
    highest = max(lowest + 1, 3 * TILES_DEV // 4)
    devcount = N_ROW * N_REP
    counts_drawn = jax.random.randint(first_key, (devcount,), lowest, highest)
    chosen = jax.random.randint(second_key, (), 0, devcount)
    return jnp.where(jnp.arange(devcount) == chosen, TILES_DEV, counts_drawn).astype(jnp.int32)


def plant(values, own_key, smallest, largest):
    longest = values.shape.index(max(values.shape))
    spots = []
    for shift in (0, 1):
        where = [jax.random.randint(jax.random.fold_in(own_key, axis), (), 0, length) for axis, length in enumerate(values.shape)]
        where[longest] = (where[longest] + shift) % values.shape[longest]
        spots.append(tuple(where))
    return values.at[spots[0]].set(smallest).at[spots[1]].set(largest)


def block_scale(rng, shape, shards, least, largest):
    level, own = 1.0, jax.random.fold_in(rng, 6)
    for axis_at, blocks in shards:
        draws = jnp.exp(jax.random.uniform(jax.random.fold_in(own, axis_at), (blocks,), jnp.float32, least / len(shards), largest / len(shards)))
        level = level * jnp.repeat(draws, shape[axis_at] // blocks).reshape([-1 if axis == axis_at else 1 for axis in range(len(shape))])
    return level


def centred(stream_key, extent, width, reach, cuts=(), kind=jnp.bfloat16):
    gain = block_scale(stream_key, extent, cuts, -0.22, 0.18) if cuts else 1.0
    drawn = jax.random.normal(stream_key, extent, jnp.float32) * width * gain
    return jnp.minimum(jnp.maximum(drawn, -reach), reach).astype(kind)


def setup_inputs(seed: int = 0) -> dict:
    arg_keys = jax.random.split(jax.random.key(seed), 8)
    features = centred(arg_keys[0], (NODES, FEAT), 1.0, 6.0, ((0, 128),), jnp.float32)
    weight = centred(arg_keys[1], (FEAT, FEAT), FEAT ** -0.5, 0.5, (), jnp.float32)
    adjacency_tiles = jnp.clip(0.05 * jax.random.uniform(arg_keys[2], (TILES, 128, 128), jnp.float32) ** block_scale(arg_keys[2], (TILES, 128, 128), ((0, 128),), -0.2, 0.2), 0.0, 0.05)
    tile_rows = plant(jax.random.randint(arg_keys[3], (TILES,), 0, ROW_TILES), jax.random.fold_in(arg_keys[3], 1), 0, ROW_TILES - 1).astype(jnp.int32)
    tile_cols = plant(jax.random.randint(arg_keys[4], (TILES,), 0, COL_TILES), jax.random.fold_in(arg_keys[4], 1), 0, COL_TILES - 1).astype(jnp.int32)
    tile_counts = draw_tile_counts(jax.random.fold_in(arg_keys[7], 71), 0)
    cluster_order = jax.vmap(lambda own: jax.random.permutation(own, SLAB))(jax.random.split(arg_keys[6], (N_ROW * N_REP))).reshape((N_ROW * N_REP, SLAB)).astype(jnp.int32)
    return dict(features=features, weight=weight, adjacency_tiles=adjacency_tiles, tile_rows=tile_rows, tile_cols=tile_cols, tile_counts=tile_counts, cluster_order=cluster_order)


def reference(features, weight, adjacency_tiles, tile_rows, tile_cols, tile_counts, cluster_order):
    devcount = N_ROW * N_REP
    slabs = features.reshape(devcount, SLAB, FEAT)
    ordered = jax.vmap(lambda slab_rows, order_rows: jnp.take(slab_rows, order_rows, axis=0))(slabs, cluster_order)
    slab_grid = ordered.reshape(N_ROW, N_REP, SLAB, FEAT)
    tiles_dev = adjacency_tiles.reshape(devcount, TILES_DEV, 128, 128)
    rows_dev = tile_rows.reshape(devcount, TILES_DEV)
    cols_dev = tile_cols.reshape(devcount, TILES_DEV)

    def device_rows(device):
        column = device % N_REP
        panel_set = lax.dynamic_index_in_dim(slab_grid, column, 1, keepdims=False)
        panel_set = panel_set.reshape(N_ROW * SLAB // 128, 128, FEAT)
        picked = panel_set[cols_dev[device]]
        products = jnp.einsum('tij,tjf->tif', tiles_dev[device], picked, precision=lax.Precision.HIGHEST)
        live_mask = (jnp.arange(TILES_DEV, dtype=jnp.int32) < tile_counts[device]).astype(products.dtype)
        products = products * live_mask[:, None, None]
        tile_sums = jax.ops.segment_sum(products, rows_dev[device], num_segments=ROW_TILES)
        return tile_sums.reshape(N_REP * SLAB, FEAT)

    partial_value = lax.map(device_rows, jnp.arange(devcount, dtype=jnp.int32))
    summed = partial_value.reshape(N_ROW, N_REP, N_REP * SLAB, FEAT).sum(axis=1).reshape(NODES, FEAT)
    mixed = jnp.dot(summed, weight, precision=lax.Precision.HIGHEST, preferred_element_type=jnp.float32)
    return jnp.maximum(mixed, 0.0)
```

```python
import functools

import jax
import jax.numpy as jnp
from jax import lax
from jax.experimental import pallas as pl
from jax.experimental.pallas import tpu as pltpu
from jax.sharding import PartitionSpec as P

MESH = pl.DeviceIdType.MESH
F32, BF16 = jnp.float32, jnp.bfloat16
T = 320
NB = 4
APIECE = 16
ASTAGE = 2
UNROLL = 40


def body(perm, pos, keep, cslot, codd, has, order, feat, weight, adj, out,
         recv, panels, aq, astage, cbuf, part, ropp, radj, rx, ordered, wb,
         g_recv, s_send, o_recv, a_recv, x_recv, a_sem):
    r, c = lax.axis_index("row"), lax.axis_index("rep")
    z, xh, kp = r // 4, (r // 2) % 2, r % 2
    y, xl = c // 2, c % 2
    zp, zm, z2 = (z + 1) % 4, (z + 3) % 4, (z + 2) % 4

    ZP = (zp * 4 + xh * 2 + kp, c)
    ZM = (zm * 4 + xh * 2 + kp, c)
    XP = (z * 4 + (1 - xh) * 2 + kp, c)
    SB = (z * 4 + xh * 2 + (1 - kp), c)
    YP = (r, ((y + 1) % 4) * 2 + xl)
    YM = (r, ((y + 3) % 4) * 2 + xl)
    XL = (r, y * 2 + (1 - xl))

    def slot(zz, xx, kk):
        return kk * 8 + zz * 2 + xx

    OWN, P0 = slot(z, xh, kp), slot(z, 1 - xh, kp)
    AP, AM, A2 = slot(zp, xh, kp), slot(zm, xh, kp), slot(z2, xh, kp)
    BP, BM, B2 = slot(zp, 1 - xh, kp), slot(zm, 1 - xh, kp), slot(z2, 1 - xh, kp)

    lane = lax.broadcasted_iota(jnp.int32, (128, 128), 1) < 64
    sends = []

    def remote(refs, target):
        k = len(sends)

        def make():
            src, dst, rsem = refs()
            return pltpu.make_async_remote_copy(
                src_ref=src, dst_ref=dst, send_sem=s_send.at[k], recv_sem=rsem,
                device_id=target, device_id_type=MESH)
        sends.append(make)
        make().start()

    def arrive(ref, rsem):
        pltpu.make_async_remote_copy(
            src_ref=ref, dst_ref=ref, send_sem=s_send.at[0], recv_sem=rsem,
            device_id=SB, device_id_type=MESH).wait_recv()

    def piece(h, s, b):
        return recv.at[h, s, pl.ds(b * 128, 128)]

    def give(h, s, b, *targets):
        for t in targets:
            remote(lambda: (piece(h, s, b), piece(h, s, b), g_recv.at[h, s, b]), t)

    def got(h, s, b):
        arrive(piece(h, s, b), g_recv.at[h, s, b])

    def convert(h, s):
        def unit(u, _):
            v = recv[h, s, pl.ds(pl.multiple_of(u * 128, 128), 128), :]
            hi = v.astype(BF16).astype(F32)
            lo = v - hi
            panels[h, s * 8 + u] = jnp.where(lane, hi, pltpu.roll(lo, 64, 1)).astype(BF16)
            panels[h, s * 8 + u + 4] = jnp.where(lane, pltpu.roll(hi, 64, 1), lo).astype(BF16)
            return 0
        lax.fori_loop(0, 4, unit, 0)

    def pack(h):
        for u in range(4):
            a = ordered[pl.ds(u * 128, 128), :]
            b = ordered[pl.ds((u + 4) * 128, 128), :]
            if h == 0:
                v = jnp.where(lane, a, pltpu.roll(b, 64, 1))
            else:
                v = jnp.where(lane, pltpu.roll(a, 64, 1), b)
            recv[h, OWN, pl.ds(u * 128, 128), :] = v

    def own_sends(h):
        for b in range(NB):
            give(h, OWN, b, XP, ZP, ZM, SB)

    def stage1(h, b):
        got(h, AM, b)
        if b < NB // 2:
            give(h, AM, b, ZP)
        got(h, AP, b)
        if b >= NB // 2:
            give(h, AP, b, ZM)
        got(h, P0, b)
        give(h, P0, b, ZP, ZM, SB)
        give(h, AM, b, SB)
        give(h, AP, b, SB)

    def stage2(h, b):
        got(h, A2, b)
        give(h, A2, b, XP, SB)
        got(h, BM, b)
        give(h, BM, b, SB)
        got(h, BP, b)
        give(h, BP, b, SB)

    def stage3(h, b):
        got(h, B2, b)
        give(h, B2, b, SB)

    def stage4(h):
        k = 1 - kp
        for s in (slot(z, xh, k), slot(z, 1 - xh, k), slot(zp, xh, k), slot(zm, xh, k),
                  slot(zp, 1 - xh, k), slot(zm, 1 - xh, k), slot(z2, xh, k), slot(z2, 1 - xh, k)):
            for b in range(NB):
                got(h, s, b)
            convert(h, s)

    def a_copy(p):
        return pltpu.make_async_copy(
            adj.at[pl.ds(p * APIECE, APIECE)], astage.at[p % ASTAGE], a_sem.at[p % ASTAGE])

    def a_piece(p):
        a_copy(p).wait()

        def tile(t, _):
            v = astage[p % ASTAGE, t]
            hi = v.astype(BF16)
            aq[p * APIECE + t, :, 0:128] = hi
            aq[p * APIECE + t, :, 128:256] = (v - hi.astype(F32)).astype(BF16)
            return 0
        lax.fori_loop(0, APIECE, tile, 0, unroll=2)
        if p + ASTAGE < T // APIECE:
            a_copy(p + ASTAGE).start()

    def compute(h, events):
        def step(i, acc):
            for u in range(UNROLL // 2):
                j = i * UNROLL + 2 * u
                w = panels[h, pos[j]]
                a0 = acc * keep[j] + jnp.dot(
                    aq[perm[j]], jnp.concatenate([w, w], 0), preferred_element_type=F32)
                w = panels[h, pos[j + 1]]
                acc = a0 * keep[j + 1] + jnp.dot(
                    aq[perm[j + 1]], jnp.concatenate([w, w], 0), preferred_element_type=F32)
                cbuf[i * (UNROLL // 2) + u] = jnp.where(lane, a0, acc) + pltpu.roll(
                    jnp.where(lane, acc, a0), 64, 1)
            for k, run in events.items():
                pl.when(i == k)(run)
            return acc
        lax.fori_loop(0, T // UNROLL, step, jnp.zeros((128, 128), F32))

    def emit(h, yo, j):
        def unit(u, _):
            e = ((yo * 2 + j) * 4 + u) * 2
            v, w = cbuf[cslot[e]], cbuf[cslot[e + 1]]
            v = jnp.where(codd[e] != 0, pltpu.roll(v, 64, 1), v) * has[e]
            w = jnp.where(codd[e + 1] != 0, w, pltpu.roll(w, 64, 1)) * has[e + 1]
            part[h, yo, j, pl.ds(pl.multiple_of(u * 128, 128), 128), :] = jnp.where(lane, v, w)
            return 0
        lax.fori_loop(0, 4, unit, 0)

    LOW, HIGH = pl.ds(0, 256), pl.ds(256, 256)

    def opp(h, j):
        emit(h, 0, j)
        remote(lambda: (part.at[h, 0, j, LOW], ropp.at[h, 0, j], o_recv.at[h, 0, j]), YP)
        remote(lambda: (part.at[h, 0, j, HIGH], ropp.at[h, 1, j], o_recv.at[h, 1, j]), YM)

    def adj_now(h, j):
        emit(h, 1, j)
        remote(lambda: (part.at[h, 1, j, HIGH], radj.at[h, 0, j, HIGH], a_recv.at[h, 0, j, 1]), YP)
        emit(h, 2, j)
        remote(lambda: (part.at[h, 2, j, LOW], radj.at[h, 1, j, LOW], a_recv.at[h, 1, j, 0]), YM)

    def adj_late(h, j):
        arrive(ropp.at[h, 0, j], o_recv.at[h, 0, j])
        part[h, 1, j, LOW] = part[h, 1, j, LOW] + ropp[h, 0, j]
        remote(lambda: (part.at[h, 1, j, LOW], radj.at[h, 0, j, LOW], a_recv.at[h, 0, j, 0]), YP)
        arrive(ropp.at[h, 1, j], o_recv.at[h, 1, j])
        part[h, 2, j, HIGH] = part[h, 2, j, HIGH] + ropp[h, 1, j]
        remote(lambda: (part.at[h, 2, j, HIGH], radj.at[h, 1, j, HIGH], a_recv.at[h, 1, j, 1]), YM)

    def own_sum(h, j, b):
        rows = (LOW, HIGH)[b]
        for d in range(2):
            arrive(radj.at[h, d, j, rows], a_recv.at[h, d, j, b])
        part[h, 3, j, rows] = part[h, 3, j, rows] + (radj[h, 0, j, rows] + radj[h, 1, j, rows])
        if j == 0:
            remote(lambda: (part.at[h, 3, 0, rows], rx.at[h, rows], x_recv.at[h, b]), XL)

    def final(h, b):
        rows = (LOW, HIGH)[b]
        arrive(rx.at[h, rows], x_recv.at[h, b])
        for u in (2 * b, 2 * b + 1):
            rr = pl.ds(u * 128, 128)
            v = part[h, 3, 1, rr] + rx[h, rr]
            hi = v.astype(BF16)
            lo = (v - hi.astype(F32)).astype(BF16)
            m = (jnp.dot(hi, wb[h, 0], preferred_element_type=F32)
                 + jnp.dot(lo, wb[h, 0], preferred_element_type=F32)
                 + jnp.dot(hi, wb[h, 1], preferred_element_type=F32))
            ra, rb = pl.ds(u * 128, 128), pl.ds((u + 4) * 128, 128)
            if h == 0:
                out[ra, :] = m[:, :128]
                out[rb, :] = m[:, 128:]
            else:
                out[ra, :] = jnp.maximum(out[ra, :] + m[:, :128], 0.0)
                out[rb, :] = jnp.maximum(out[rb, :] + m[:, 128:], 0.0)

    for p in range(ASTAGE):
        a_copy(p).start()
    barrier = pltpu.get_barrier_semaphore()
    around = (ZP, ZM, XP, SB, YP, YM, XL)
    for t in around:
        pl.semaphore_signal(barrier, inc=1, device_id=t, device_id_type=MESH)

    def take(i, _):
        for k in range(16):
            ordered[pl.ds(i * 16 + k, 1), :] = feat[pl.ds(order[i * 16 + k], 1), :]
        return 0
    lax.fori_loop(0, 64, take, 0)
    pack(0)
    pl.semaphore_wait(barrier, len(around))
    own_sends(0)
    pack(1)
    convert(0, OWN)
    convert(1, OWN)
    wb[...] = jnp.zeros_like(wb)
    for h in range(2):
        w = weight[pl.ds(h * 64, 64), :]
        hi = w.astype(BF16)
        for k, v in enumerate((hi, (w - hi.astype(F32)).astype(BF16))):
            wb[h, k, 0:64, 0:128] = v
            wb[h, k, 64:128, 128:256] = v

    pieces = list(range(T // APIECE))
    for p in pieces[:6]:
        a_piece(p)
    todo = pieces[6:]
    for b in range(NB):
        stage1(0, b)
        for p in todo[3 * b:3 * b + 3]:
            a_piece(p)
    for s in (P0, AM, AP):
        convert(0, s)
    for b in range(NB):
        stage2(0, b)
        for p in todo[12 + b:13 + b]:
            a_piece(p)
    own_sends(1)
    for s in (A2, BM, BP):
        convert(0, s)
    for b in range(NB):
        stage3(0, b)
    convert(0, B2)
    stage4(0)

    compute(0, {1 + 2 * b: functools.partial(stage1, 1, b) for b in range(NB)})
    for j in range(2):
        opp(0, j)
    for j in range(2):
        adj_now(0, j)
    for b in range(NB):
        stage2(1, b)
    for j in range(2):
        adj_late(0, j)
    for j in range(2):
        emit(0, 3, j)
    for s in (P0, AM, AP, A2, BM, BP):
        convert(1, s)
    for b in range(NB):
        stage3(1, b)
    convert(1, B2)
    stage4(1)

    compute(1, {})
    for j in range(2):
        opp(1, j)
    for j in range(2):
        adj_now(1, j)
    for b in (1, 0):
        own_sum(0, 0, b)
    for j in range(2):
        adj_late(1, j)
    for j in range(2):
        emit(1, 3, j)
    for b in (1, 0):
        own_sum(0, 1, b)
        final(0, b)
    for j in range(2):
        for b in (1, 0):
            own_sum(1, j, b)
    for b in (1, 0):
        final(1, b)
    for make in sends:
        make().wait_send()


N_SEND = 2 * (15 * NB + 14)


def shards(features, weight, adjacency_tiles, tile_rows, tile_cols, tile_counts, cluster_order):
    c = lax.axis_index("rep")
    y, xl = c // 2, c % 2
    j = jnp.arange(T, dtype=jnp.int32)
    dy, rx_, t = (tile_rows // 16 - y) % 4, (tile_rows // 8) % 2, tile_rows % 8
    yo = jnp.where(dy == 0, 3, jnp.where(dy == 1, 1, jnp.where(dy == 2, 0, 2)))
    rel = ((yo * 2 + (rx_ == xl)) * 4 + t % 4) * 2 + t // 4
    key = jnp.where(j < tile_counts[0], rel, 64)
    k = tile_cols // 8
    place = ((k % 2) * 8 + k // 2) * 8 + tile_cols % 8
    code = key * 65536 + place * 512 + j
    rank = jnp.sum((code[None, :] < code[:, None]).astype(jnp.int32), axis=1)
    code = jnp.sum(jnp.where(rank[:, None] == j[None, :], code[:, None], 0), axis=0)
    perm, pos, row = code % 512, (code // 512) % 128, code // 65536
    keep = jnp.concatenate([jnp.zeros((1,), F32), (row[1:] == row[:-1]).astype(F32)])
    upto = jnp.sum((key[None, :] <= jnp.arange(-1, 64, dtype=jnp.int32)[:, None]).astype(jnp.int32), axis=1)
    has = (upto[1:] > upto[:-1]).astype(F32)
    last = jnp.maximum(upto[1:] - 1, 0)
    smem = pl.BlockSpec(memory_space=pltpu.SMEM)
    vmem = pl.BlockSpec(memory_space=pltpu.VMEM)
    dma = pltpu.SemaphoreType.DMA
    return pl.pallas_call(
        body,
        out_shape=jax.ShapeDtypeStruct((1024, 128), F32),
        in_specs=[smem] * 7 + [vmem, vmem, pl.BlockSpec(memory_space=pl.ANY)],
        out_specs=vmem,
        scratch_shapes=[
            pltpu.VMEM((2, 16, 512, 128), F32),
            pltpu.VMEM((2, 128, 128, 128), BF16),
            pltpu.VMEM((T, 128, 256), BF16),
            pltpu.VMEM((ASTAGE, APIECE, 128, 128), F32),
            pltpu.VMEM((T // 2, 128, 128), F32),
            pltpu.VMEM((2, 4, 2, 512, 128), F32),
            pltpu.VMEM((2, 2, 2, 256, 128), F32),
            pltpu.VMEM((2, 2, 2, 512, 128), F32),
            pltpu.VMEM((2, 512, 128), F32),
            pltpu.VMEM((1024, 128), F32),
            pltpu.VMEM((2, 2, 128, 256), BF16),
            dma((2, 16, NB)),
            dma((N_SEND,)),
            dma((2, 2, 2)),
            dma((2, 2, 2, 2)),
            dma((2, 2)),
            dma((ASTAGE,)),
        ],
        compiler_params=pltpu.CompilerParams(
            collective_id=0, has_side_effects=True, vmem_limit_bytes=63 * 1024 * 1024),
    )(perm, pos, keep, last // 2, last % 2, has, cluster_order[0], features, weight, adjacency_tiles)


def solution(mesh):
    placed = (
        P(("row", "rep"), None),
        P(),
        P(("row", "rep"), None, None),
        P(("row", "rep")),
        P(("row", "rep")),
        P(("row", "rep")),
        P(("row", "rep"), None),
    )
    return jax.shard_map(
        shards, mesh=mesh, in_specs=placed, out_specs=P(("row", "rep"), None), check_vma=False
    )
```

```python
import functools

import jax
import jax.numpy as jnp
from jax import lax
from jax.experimental import pallas as pl
from jax.experimental.pallas import tpu as pltpu
from jax.sharding import PartitionSpec as P

MESH = pl.DeviceIdType.MESH
F32, BF16 = jnp.float32, jnp.bfloat16
T = 320
NB = 4
APIECE = 16
ASTAGE = 4
UNROLL = 64


def body(order, code, feat, weight, adj, out,
         recv, panels, aq, astage, cbuf, part, ropp, radj, rx, ordered, wb,
         ivec, fvec, itab, ftab, g_recv, s_send, o_recv, a_recv, x_recv, a_sem, t_sem):
    r, c = lax.axis_index("row"), lax.axis_index("rep")
    z, xh, kp = r // 4, (r // 2) % 2, r % 2
    y, xl = c // 2, c % 2
    zp, zm, z2 = (z + 1) % 4, (z + 3) % 4, (z + 2) % 4

    ZP = (zp * 4 + xh * 2 + kp, c)
    ZM = (zm * 4 + xh * 2 + kp, c)
    XP = (z * 4 + (1 - xh) * 2 + kp, c)
    SB = (z * 4 + xh * 2 + (1 - kp), c)
    YP = (r, ((y + 1) % 4) * 2 + xl)
    YM = (r, ((y + 3) % 4) * 2 + xl)
    XL = (r, y * 2 + (1 - xl))

    def slot(zz, xx, kk):
        return kk * 8 + zz * 2 + xx

    OWN, P0 = slot(z, xh, kp), slot(z, 1 - xh, kp)
    AP, AM, A2 = slot(zp, xh, kp), slot(zm, xh, kp), slot(z2, xh, kp)
    BP, BM, B2 = slot(zp, 1 - xh, kp), slot(zm, 1 - xh, kp), slot(z2, 1 - xh, kp)

    lane = lax.broadcasted_iota(jnp.int32, (128, 128), 1) < 64
    sends = []

    def remote(refs, target):
        k = len(sends)

        def make():
            src, dst, rsem = refs()
            return pltpu.make_async_remote_copy(
                src_ref=src, dst_ref=dst, send_sem=s_send.at[k], recv_sem=rsem,
                device_id=target, device_id_type=MESH)
        sends.append(make)
        make().start()

    def arrive(ref, rsem):
        pltpu.make_async_remote_copy(
            src_ref=ref, dst_ref=ref, send_sem=s_send.at[0], recv_sem=rsem,
            device_id=SB, device_id_type=MESH).wait_recv()

    def piece(h, s, b):
        return recv.at[h, s, pl.ds(b * 128, 128)]

    def give(h, s, b, *targets):
        for t in targets:
            remote(lambda: (piece(h, s, b), piece(h, s, b), g_recv.at[h, s, b]), t)

    def got(h, s, b):
        arrive(piece(h, s, b), g_recv.at[h, s, b])

    def convert(h, s):
        def unit(u, _):
            v = recv[h, s, pl.ds(pl.multiple_of(u * 128, 128), 128), :]
            hi = v.astype(BF16)
            panels[h, s * 4 + u, :, 0:128] = hi
            panels[h, s * 4 + u, :, 128:256] = (v - hi.astype(F32)).astype(BF16)
            return 0
        lax.fori_loop(0, 4, unit, 0, unroll=2)

    def pack(h, u):
        a = ordered[pl.ds(u * 128, 128), :]
        b = ordered[pl.ds((u + 4) * 128, 128), :]
        if h == 0:
            v = jnp.where(lane, a, pltpu.roll(b, 64, 1))
        else:
            v = jnp.where(lane, pltpu.roll(a, 64, 1), b)
        recv[h, OWN, pl.ds(u * 128, 128), :] = v

    def own_sends(h, b):
        give(h, OWN, b, (ZP, ZM)[b % 2], XP, SB)
        if b == NB - 1:
            for k in range(NB):
                give(h, OWN, k, (ZM, ZP)[k % 2])

    def relay(h, b):
        got(h, AM, b)
        give(h, AM, b, ZP, SB)
        got(h, AP, b + 1)
        give(h, AP, b + 1, ZM, SB)

    def across(h, b):
        got(h, P0, b)
        give(h, P0, b, ZP, ZM, SB)

    def rest(h, b):
        got(h, AM, b + 1)
        give(h, AM, b + 1, SB)
        got(h, AP, b)
        give(h, AP, b, SB)

    def stage2(h, b):
        got(h, A2, b)
        give(h, A2, b, XP, SB)

    def stage2b(h, b):
        got(h, BM, b)
        give(h, BM, b, SB)
        got(h, BP, b)
        give(h, BP, b, SB)

    def stage3(h, b):
        got(h, B2, b)
        give(h, B2, b, SB)

    def stage4(h):
        k = 1 - kp
        for s in (slot(z, xh, k), slot(z, 1 - xh, k), slot(zp, xh, k), slot(zm, xh, k),
                  slot(z2, xh, k), slot(zp, 1 - xh, k), slot(zm, 1 - xh, k), slot(z2, 1 - xh, k)):
            for b in range(NB):
                got(h, s, b)
            convert(h, s)

    def a_copy(p):
        return pltpu.make_async_copy(
            adj.at[pl.ds(p * APIECE, APIECE)], astage.at[p % ASTAGE], a_sem.at[p % ASTAGE])

    def a_piece(p):
        a_copy(p).wait()

        def tile(t, _):
            v = astage[p % ASTAGE, t]
            hi = v.astype(BF16)
            aq[p * APIECE + t, :, 0:128] = hi
            aq[p * APIECE + t, :, 128:256] = (v - hi.astype(F32)).astype(BF16)
            return 0
        lax.fori_loop(0, APIECE, tile, 0, unroll=2)
        if p + ASTAGE < T // APIECE:
            a_copy(p + ASTAGE).start()

    def compute(h, events):
        low = lax.broadcasted_iota(jnp.int32, (1, 128), 1) < 64

        def step(i, acc):
            row, col = i // (128 // UNROLL), (i % (128 // UNROLL)) * UNROLL

            def add(u, acc):
                w = panels[h, itab[3 + row, col + u]]
                p = jnp.dot(aq[itab[row, col + u]], jnp.concatenate([w, w], 0),
                            preferred_element_type=F32)
                side = jnp.where(low, ftab[3 + row, col + u], ftab[6 + row, col + u])
                return acc * ftab[row, col + u] + (p[:, :128] + p[:, 128:]) * side

            for u in range(0, UNROLL, 2):
                a0 = add(u, acc)
                acc = add(u + 1, a0)
                cbuf[i * (UNROLL // 2) + u // 2] = jnp.where(lane, a0, acc) + pltpu.roll(
                    jnp.where(lane, acc, a0), 64, 1)
            for k, run in events.items():
                pl.when(i == k)(run)
            return acc
        lax.fori_loop(0, T // UNROLL, step, jnp.zeros((128, 128), F32))

    def emit(h, yo, j):
        low = lax.broadcasted_iota(jnp.int32, (1, 128), 1) < 64

        def unit(u, _):
            e = ((yo * 2 + j) * 4 + u) * 2
            v, w = cbuf[itab[6, e]], cbuf[itab[6, e + 1]]
            stay = jnp.where(low, ftab[9, e], ftab[10, e + 1])
            turn = jnp.where(low, ftab[10, e], ftab[9, e + 1])
            part[h, yo, j, pl.ds(pl.multiple_of(u * 128, 128), 128), :] = (
                jnp.where(lane, v, w) * stay + pltpu.roll(jnp.where(lane, w, v), 64, 1) * turn)
            return 0
        lax.fori_loop(0, 4, unit, 0, unroll=4)

    def tables():
        def down(v):
            return jnp.transpose(jnp.broadcast_to(v, (128, 128)))

        def total(v):
            return jnp.sum(v, axis=0, keepdims=True)
        at = lax.broadcasted_iota(jnp.int32, (1, 128), 1)
        rows = [code[pl.ds(k, 1), :] for k in range(3)]
        cols = [down(v) for v in rows]
        ranks = [down(sum(total((m < v).astype(jnp.int32)) for m in cols)) for v in rows]
        for k in range(3):
            here = sum(total(jnp.where(n == at + k * 128, m, 0)) for n, m in zip(ranks, cols))
            back = sum(total(jnp.where(n == at + (k * 128 - 1), m, 0)) for n, m in zip(ranks, cols))
            side = (here // 32768) % 2
            ivec[pl.ds(k, 1), :] = jnp.minimum(here % 512, T - 1)
            ivec[pl.ds(3 + k, 1), :] = (here // 512) % 64
            fvec[pl.ds(k, 1), :] = (here // 65536 == back // 65536).astype(F32)
            fvec[pl.ds(3 + k, 1), :] = (1 - side).astype(F32)
            fvec[pl.ds(6 + k, 1), :] = side.astype(F32)
        upto = sum(total((m // 65536 <= at).astype(jnp.int32)) for m in cols)
        before = sum(total((m // 65536 < at).astype(jnp.int32)) for m in cols)
        last = jnp.clip(upto - 1, 0, T - 1)
        has = jnp.where(upto > before, 1, 0)
        ivec[pl.ds(6, 1), :] = last // 2
        fvec[pl.ds(9, 1), :] = (has * (1 - last % 2)).astype(F32)
        fvec[pl.ds(10, 1), :] = (has * (last % 2)).astype(F32)

    def table_copies():
        return (pltpu.make_async_copy(ivec, itab, t_sem.at[0]),
                pltpu.make_async_copy(fvec, ftab, t_sem.at[1]))

    LOW, HIGH = pl.ds(0, 256), pl.ds(256, 256)

    def opp(h, j):
        emit(h, 0, j)
        remote(lambda: (part.at[h, 0, j, LOW], ropp.at[h, 0, j], o_recv.at[h, 0, j]), YP)
        remote(lambda: (part.at[h, 0, j, HIGH], ropp.at[h, 1, j], o_recv.at[h, 1, j]), YM)

    def adj_now(h, j):
        emit(h, 1, j)
        remote(lambda: (part.at[h, 1, j, HIGH], radj.at[h, 0, j, HIGH], a_recv.at[h, 0, j, 1]), YP)
        emit(h, 2, j)
        remote(lambda: (part.at[h, 2, j, LOW], radj.at[h, 1, j, LOW], a_recv.at[h, 1, j, 0]), YM)

    def adj_late(h, j):
        arrive(ropp.at[h, 0, j], o_recv.at[h, 0, j])
        part[h, 1, j, LOW] = part[h, 1, j, LOW] + ropp[h, 0, j]
        remote(lambda: (part.at[h, 1, j, LOW], radj.at[h, 0, j, LOW], a_recv.at[h, 0, j, 0]), YP)
        arrive(ropp.at[h, 1, j], o_recv.at[h, 1, j])
        part[h, 2, j, HIGH] = part[h, 2, j, HIGH] + ropp[h, 1, j]
        remote(lambda: (part.at[h, 2, j, HIGH], radj.at[h, 1, j, HIGH], a_recv.at[h, 1, j, 1]), YM)

    def own_sum(h, j, b):
        rows = (LOW, HIGH)[b]
        for d in range(2):
            arrive(radj.at[h, d, j, rows], a_recv.at[h, d, j, b])
        part[h, 3, j, rows] = part[h, 3, j, rows] + (radj[h, 0, j, rows] + radj[h, 1, j, rows])
        if j == 0:
            remote(lambda: (part.at[h, 3, 0, rows], rx.at[h, rows], x_recv.at[h, b]), XL)

    def final(h, b):
        rows = (LOW, HIGH)[b]
        arrive(rx.at[h, rows], x_recv.at[h, b])
        for u in (2 * b, 2 * b + 1):
            rr = pl.ds(u * 128, 128)
            v = part[h, 3, 1, rr] + rx[h, rr]
            hi = v.astype(BF16)
            lo = (v - hi.astype(F32)).astype(BF16)
            m = (jnp.dot(hi, wb[h, 0], preferred_element_type=F32)
                 + jnp.dot(lo, wb[h, 0], preferred_element_type=F32)
                 + jnp.dot(hi, wb[h, 1], preferred_element_type=F32))
            ra, rb = pl.ds(u * 128, 128), pl.ds((u + 4) * 128, 128)
            if h == 0:
                out[ra, :] = m[:, :128]
                out[rb, :] = m[:, 128:]
            else:
                out[ra, :] = jnp.maximum(out[ra, :] + m[:, :128], 0.0)
                out[rb, :] = jnp.maximum(out[rb, :] + m[:, 128:], 0.0)

    barrier = pltpu.get_barrier_semaphore()
    around = (ZP, ZM, XP, SB, YP, YM, XL)
    for t in around:
        pl.semaphore_signal(barrier, inc=1, device_id=t, device_id_type=MESH)
    for p in range(ASTAGE):
        a_copy(p).start()

    for u in range(NB):
        for o in (u, u + 4):
            def take(i, _):
                for k in range(16):
                    at = o * 128 + i * 16 + k
                    ordered[pl.ds(at, 1), :] = feat[pl.ds(order[0, at], 1), :]
                return 0
            lax.fori_loop(0, 8, take, 0)
        pack(0, u)
        if u == 0:
            pl.semaphore_wait(barrier, len(around))
        own_sends(0, u)
    ivec[...] = jnp.zeros_like(ivec)
    fvec[...] = jnp.zeros_like(fvec)
    tables()
    for copy in table_copies():
        copy.start()

    todo = iter(range(T // APIECE))

    def a_pieces(n):
        for _ in range(n):
            p = next(todo, None)
            if p is not None:
                a_piece(p)

    a_pieces(2)
    relay(0, 0)
    a_pieces(2)
    across(0, 0)
    relay(0, 2)
    a_pieces(2)
    for b in range(1, NB):
        across(0, b)
        a_pieces(1)
    for u in range(4):
        pack(1, u)
    for h in range(2):
        convert(h, OWN)
    wb[...] = jnp.zeros_like(wb)
    for h in range(2):
        w = weight[pl.ds(h * 64, 64), :]
        hi = w.astype(BF16)
        for k, v in enumerate((hi, (w - hi.astype(F32)).astype(BF16))):
            wb[h, k, 0:64, 0:128] = v
            wb[h, k, 64:128, 128:256] = v
    for b in (0, 2):
        rest(0, b)
        a_pieces(1)
    for b in range(NB):
        stage2(0, b)
        a_pieces(1)
    for s in (P0, AM, AP, A2):
        convert(0, s)
        a_pieces(1)
    for b in range(NB):
        stage2b(0, b)
        own_sends(1, b)
        a_pieces(1)
    for s in (BM, BP):
        convert(0, s)
    for b in range(NB):
        stage3(0, b)
    convert(0, B2)
    for copy in table_copies():
        copy.wait()
    stage4(0)

    def both(*runs):
        def go():
            for f, *args in runs:
                f(*args)
        return go

    compute(0, {
        0: both((relay, 1, 0)),
        1: both((across, 1, 0), (relay, 1, 2)),
        2: both((across, 1, 1)),
        3: both((across, 1, 2), (rest, 1, 0)),
        4: both((across, 1, 3), (rest, 1, 2)),
    })
    for j in range(2):
        opp(0, j)
        adj_now(0, j)
    for b in range(NB):
        stage2(1, b)
    for j in range(2):
        adj_late(0, j)
    for j in range(2):
        emit(0, 3, j)
    for s in (P0, AM, AP, A2):
        convert(1, s)
    for b in range(NB):
        stage2b(1, b)
    for s in (BM, BP):
        convert(1, s)
    for b in range(NB):
        stage3(1, b)
    convert(1, B2)
    stage4(1)

    compute(1, {
        3: both((own_sum, 0, 0, 1)),
        4: both((own_sum, 0, 0, 0)),
    })
    opp(1, 0)
    adj_now(1, 0)
    opp(1, 1)
    adj_now(1, 1)
    emit(1, 3, 0)
    emit(1, 3, 1)
    for b in (1, 0):
        own_sum(0, 1, b)
    adj_late(1, 0)
    for b in (1, 0):
        final(0, b)
    adj_late(1, 1)
    for j in range(2):
        for b in (1, 0):
            own_sum(1, j, b)
    for b in (1, 0):
        final(1, b)
    for make in sends:
        make().wait_send()


N_SEND = 2 * (15 * NB + 14)


def shards(features, weight, adjacency_tiles, tile_rows, tile_cols, tile_counts, cluster_order):
    c = lax.axis_index("rep")
    y, xl = c // 2, c % 2
    j = jnp.arange(T, dtype=jnp.int32)
    dy, rx_, t = (tile_rows // 16 - y) % 4, (tile_rows // 8) % 2, tile_rows % 8
    yo = jnp.where(dy == 0, 3, jnp.where(dy == 1, 1, jnp.where(dy == 2, 0, 2)))
    rel = ((yo * 2 + (rx_ == xl)) * 4 + t % 4) * 2 + t // 4
    key = jnp.where(j < tile_counts[0], rel, 64)
    k, o = tile_cols // 8, tile_cols % 8
    panel = ((k % 2) * 8 + k // 2) * 4 + o % 4
    code = key * 65536 + (o // 4) * 32768 + panel * 512 + j
    more = jnp.arange(T, 384, dtype=jnp.int32) + 64 * 65536
    code = jnp.concatenate([code, more]).reshape(3, 128)
    smem = pl.BlockSpec(memory_space=pltpu.SMEM)
    vmem = pl.BlockSpec(memory_space=pltpu.VMEM)
    dma = pltpu.SemaphoreType.DMA
    return pl.pallas_call(
        body,
        out_shape=jax.ShapeDtypeStruct((1024, 128), F32),
        in_specs=[smem, vmem, vmem, vmem, pl.BlockSpec(memory_space=pl.ANY)],
        out_specs=vmem,
        scratch_shapes=[
            pltpu.VMEM((2, 16, 512, 128), F32),
            pltpu.VMEM((2, 64, 128, 256), BF16),
            pltpu.VMEM((T, 128, 256), BF16),
            pltpu.VMEM((ASTAGE, APIECE, 128, 128), F32),
            pltpu.VMEM((T // 2, 128, 128), F32),
            pltpu.VMEM((2, 4, 2, 512, 128), F32),
            pltpu.VMEM((2, 2, 2, 256, 128), F32),
            pltpu.VMEM((2, 2, 2, 512, 128), F32),
            pltpu.VMEM((2, 512, 128), F32),
            pltpu.VMEM((1024, 128), F32),
            pltpu.VMEM((2, 2, 128, 256), BF16),
            pltpu.VMEM((16, 128), jnp.int32),
            pltpu.VMEM((16, 128), F32),
            pltpu.SMEM((16, 128), jnp.int32),
            pltpu.SMEM((16, 128), F32),
            dma((2, 16, NB)),
            dma((N_SEND,)),
            dma((2, 2, 2)),
            dma((2, 2, 2, 2)),
            dma((2, 2)),
            dma((ASTAGE,)),
            dma((2,)),
        ],
        compiler_params=pltpu.CompilerParams(
            collective_id=0, has_side_effects=True, vmem_limit_bytes=63 * 1024 * 1024),
    )(cluster_order, code, features, weight, adjacency_tiles)


def solution(mesh):
    placed = (
        P(("row", "rep"), None),
        P(),
        P(("row", "rep"), None, None),
        P(("row", "rep")),
        P(("row", "rep")),
        P(("row", "rep")),
        P(("row", "rep"), None),
    )
    return jax.shard_map(
        shards, mesh=mesh, in_specs=placed, out_specs=P(("row", "rep"), None), check_vma=False
    )
```

```python
import functools

import jax
import jax.numpy as jnp
from jax import lax
from jax.experimental import pallas as pl
from jax.experimental.pallas import tpu as pltpu
from jax.sharding import PartitionSpec as P

MESH = pl.DeviceIdType.MESH
F32, BF16 = jnp.float32, jnp.bfloat16
T = 320
NB = 4
APIECE = 16
ASTAGE = 4
UNROLL = 64
FY = 384


def body(order, code, feat, weight, adj, out,
         recv, panels, aq, astage, cbuf, part, first, ropp, radj, rx, ordered, wb,
         ivec, fvec, itab, ftab, g_recv, c_recv, s_send, f_recv, o_recv, a_recv, x_recv, a_sem, t_sem):
    r, c = lax.axis_index("row"), lax.axis_index("rep")
    z, xh, kp = r // 4, (r // 2) % 2, r % 2
    y, xl = c // 2, c % 2
    zp, zm, z2 = (z + 1) % 4, (z + 3) % 4, (z + 2) % 4

    ZP = (zp * 4 + xh * 2 + kp, c)
    ZM = (zm * 4 + xh * 2 + kp, c)
    XP = (z * 4 + (1 - xh) * 2 + kp, c)
    SB = (z * 4 + xh * 2 + (1 - kp), c)
    YP = (r, ((y + 1) % 4) * 2 + xl)
    YM = (r, ((y + 3) % 4) * 2 + xl)
    XL = (r, y * 2 + (1 - xl))

    def slot(zz, xx, kk):
        return kk * 8 + zz * 2 + xx

    OWN, P0 = slot(z, xh, kp), slot(z, 1 - xh, kp)
    AP, AM, A2 = slot(zp, xh, kp), slot(zm, xh, kp), slot(z2, xh, kp)
    BP, BM, B2 = slot(zp, 1 - xh, kp), slot(zm, 1 - xh, kp), slot(z2, 1 - xh, kp)

    lane = lax.broadcasted_iota(jnp.int32, (128, 128), 1) < 64
    def remote(src, dst, ssem, rsem, target):
        pltpu.make_async_remote_copy(
            src_ref=src, dst_ref=dst, send_sem=ssem, recv_sem=rsem,
            device_id=target, device_id_type=MESH).start()

    def arrive(ref, rsem):
        pltpu.make_async_remote_copy(
            src_ref=ref, dst_ref=ref, send_sem=s_send.at[0], recv_sem=rsem,
            device_id=SB, device_id_type=MESH).wait_recv()

    def sent(ref, ssem):
        pltpu.make_async_remote_copy(
            src_ref=ref, dst_ref=ref, send_sem=ssem, recv_sem=f_recv.at[0],
            device_id=SB, device_id_type=MESH).wait_send()

    def piece(h, s, b):
        return recv.at[h, s, pl.ds(b * 128, 128)]

    def give(h, s, b, *targets):
        for t in targets:
            there = c_recv.at[h, s % 8] if t is SB else g_recv.at[h, s % 8, b]
            remote(piece(h, s, b), piece(h, s, b), s_send.at[h], there, t)

    def got(h, s, b):
        arrive(piece(h, s, b), g_recv.at[h, s % 8, b])

    def convert(h, s):
        def unit(u, _):
            v = recv[h, s, pl.ds(pl.multiple_of(u * 128, 128), 128), :]
            hi = v.astype(BF16)
            panels[h, s * 4 + u, :, 0:128] = hi
            panels[h, s * 4 + u, :, 128:256] = (v - hi.astype(F32)).astype(BF16)
            return 0
        lax.fori_loop(0, 4, unit, 0, unroll=2)

    def pack(h, u):
        a = ordered[pl.ds(u * 128, 128), :]
        b = ordered[pl.ds((u + 4) * 128, 128), :]
        if h == 0:
            v = jnp.where(lane, a, pltpu.roll(b, 64, 1))
        else:
            v = jnp.where(lane, pltpu.roll(a, 64, 1), b)
        recv[h, OWN, pl.ds(u * 128, 128), :] = v

    def start(h):
        for b in (0, 2):
            give(h, OWN, b, ZP)
            give(h, OWN, b + 1, ZM)
        for b in (0, 1):
            give(h, OWN, b, XP)

    def more(h):
        for b in (2, 3):
            give(h, OWN, b, XP)
        for b in range(NB):
            give(h, OWN, b, SB)

    def fill(h, b):
        give(h, OWN, b + 1, ZP)
        give(h, OWN, b, ZM)

    def relay(h, b):
        got(h, AM, b)
        give(h, AM, b, ZP, SB)
        got(h, AP, b + 1)
        give(h, AP, b + 1, ZM, SB)

    def across(h, b):
        got(h, P0, b)
        give(h, P0, b, ZP, ZM, SB)

    def rest(h, b):
        got(h, AM, b + 1)
        give(h, AM, b + 1, SB)
        got(h, AP, b)
        give(h, AP, b, SB)

    def stage2(h, b):
        got(h, A2, b)
        give(h, A2, b, XP, SB)

    def stage2b(h, b):
        got(h, BM, b)
        give(h, BM, b, SB)
        got(h, BP, b)
        give(h, BP, b, SB)

    def stage3(h, b):
        got(h, B2, b)
        give(h, B2, b, SB)

    def stage4(h):
        k = 1 - kp
        for s in (slot(z, xh, k), slot(z, 1 - xh, k), slot(zp, xh, k), slot(zm, xh, k),
                  slot(z2, xh, k), slot(zp, 1 - xh, k), slot(zm, 1 - xh, k), slot(z2, 1 - xh, k)):
            arrive(recv.at[h, s], c_recv.at[h, s % 8])
            convert(h, s)

    def a_copy(p):
        return pltpu.make_async_copy(
            adj.at[pl.ds(p * APIECE, APIECE)], astage.at[p % ASTAGE], a_sem.at[p % ASTAGE])

    def a_piece(p):
        a_copy(p).wait()

        def tile(t, _):
            v = astage[p % ASTAGE, t]
            hi = v.astype(BF16)
            aq[p * APIECE + t, :, 0:128] = hi
            aq[p * APIECE + t, :, 128:256] = (v - hi.astype(F32)).astype(BF16)
            return 0
        lax.fori_loop(0, APIECE, tile, 0, unroll=2)
        if p + ASTAGE < T // APIECE:
            a_copy(p + ASTAGE).start()

    def compute(h, events):
        low = lax.broadcasted_iota(jnp.int32, (1, 128), 1) < 64

        def step(i, acc):
            row, col = i // (128 // UNROLL), (i % (128 // UNROLL)) * UNROLL

            def add(u, acc):
                w = panels[h, itab[3 + row, col + u]]
                p = jnp.dot(aq[itab[row, col + u]], jnp.concatenate([w, w], 0),
                            preferred_element_type=F32)
                side = jnp.where(low, ftab[3 + row, col + u], ftab[6 + row, col + u])
                return acc * ftab[row, col + u] + (p[:, :128] + p[:, 128:]) * side

            for u in range(0, UNROLL, 2):
                a0 = add(u, acc)
                acc = add(u + 1, a0)
                cbuf[i * (UNROLL // 2) + u // 2] = jnp.where(lane, a0, acc) + pltpu.roll(
                    jnp.where(lane, acc, a0), 64, 1)
            for k, run in events.items():
                pl.when(i == k)(run)
            return acc
        lax.fori_loop(0, T // UNROLL, step, jnp.zeros((128, 128), F32))

    def emit(h, yo, j, units=range(4)):
        low = lax.broadcasted_iota(jnp.int32, (1, 128), 1) < 64
        for u in units:
            e = ((yo * 2 + j) * 4 + u) * 2
            v, w = cbuf[itab[6, e]], cbuf[itab[6, e + 1]]
            stay = jnp.where(low, ftab[9, e], ftab[10, e + 1])
            turn = jnp.where(low, ftab[10, e], ftab[9, e + 1])
            part[h, yo, j, pl.ds(u * 128, 128), :] = (
                jnp.where(lane, v, w) * stay + pltpu.roll(jnp.where(lane, w, v), 64, 1) * turn)

    def tables():
        def down(v):
            return jnp.transpose(jnp.broadcast_to(v, (128, 128)))

        def total(v):
            return jnp.sum(v, axis=0, keepdims=True)
        at = lax.broadcasted_iota(jnp.int32, (1, 128), 1)
        rows = [code[pl.ds(k, 1), :] for k in range(3)]
        cols = [down(v) for v in rows]
        ranks = [down(sum(total((m < v).astype(jnp.int32)) for m in cols)) for v in rows]
        for k in range(3):
            here = sum(total(jnp.where(n == at + k * 128, m, 0)) for n, m in zip(ranks, cols))
            back = sum(total(jnp.where(n == at + (k * 128 - 1), m, 0)) for n, m in zip(ranks, cols))
            side = (here // 32768) % 2
            ivec[pl.ds(k, 1), :] = jnp.minimum(here % 512, T - 1)
            ivec[pl.ds(3 + k, 1), :] = (here // 512) % 64
            fvec[pl.ds(k, 1), :] = (here // 65536 == back // 65536).astype(F32)
            fvec[pl.ds(3 + k, 1), :] = (1 - side).astype(F32)
            fvec[pl.ds(6 + k, 1), :] = side.astype(F32)
        upto = sum(total((m // 65536 <= at).astype(jnp.int32)) for m in cols)
        before = sum(total((m // 65536 < at).astype(jnp.int32)) for m in cols)
        last = jnp.clip(upto - 1, 0, T - 1)
        has = jnp.where(upto > before, 1, 0)
        ivec[pl.ds(6, 1), :] = last // 2
        fvec[pl.ds(9, 1), :] = (has * (1 - last % 2)).astype(F32)
        fvec[pl.ds(10, 1), :] = (has * (last % 2)).astype(F32)

    def table_copies():
        return (pltpu.make_async_copy(ivec, itab, t_sem.at[0]),
                pltpu.make_async_copy(fvec, ftab, t_sem.at[1]))

    LATE = pl.ds(FY, 512 - FY)

    def half(j, b):
        n = FY // 2 if j < 2 else (512 - FY) // 2
        return min(j, 1), pl.ds((FY if j == 2 else 0) + b * n, n), pl.ds(0, n)

    def first_x(h):
        for yo in range(4):
            emit(h, yo, 0, range(FY // 128, 4))
        remote(part.at[h, :, 0, LATE], first.at[h], s_send.at[2 + h], f_recv.at[h], XL)

    def first_add(h):
        arrive(first.at[h], f_recv.at[h])
        for yo in range(4):
            part[h, yo, 1, LATE] = part[h, yo, 1, LATE] + first[h, yo]
        now(h, 2)

    def adj_send(h, j, d, b):
        k, rows, _ = half(j, b)
        remote(part.at[h, 1 + d, k, rows], radj.at[h, d, k, rows],
               s_send.at[2 + h], a_recv.at[h, d, j, b], (YP, YM)[d])

    def now(h, j):
        for d in range(2):
            k, rows, there = half(j, d)
            if j < 2:
                emit(h, 0, k, range(0 if d == 0 else 2, 2 if d == 0 else 3))
            remote(part.at[h, 0, k, rows], ropp.at[h, d, j, there],
                   s_send.at[2 + h], o_recv.at[h, d, j], (YP, YM)[d])
        for d in range(2):
            if j < 2:
                emit(h, 1 + d, k, range(FY // 128))
            adj_send(h, j, d, 1 - d)

    def adj_late(h, j):
        for d in range(2):
            k, rows, there = half(j, d)
            arrive(ropp.at[h, d, j, there], o_recv.at[h, d, j])
            part[h, 1 + d, k, rows] = part[h, 1 + d, k, rows] + ropp[h, d, j, there]
            adj_send(h, j, d, d)

    def own_sum(h, j):
        for b in (1, 0):
            k, rows, _ = half(j, b)
            for d in range(2):
                arrive(radj.at[h, d, k, rows], a_recv.at[h, d, j, b])
            part[h, 3, k, rows] = part[h, 3, k, rows] + (radj[h, 0, k, rows] + radj[h, 1, k, rows])
            if j == 0:
                remote(part.at[h, 3, 0, rows], rx.at[h, rows], s_send.at[2 + h], x_recv.at[h, b], XL)

    def sums_start(h):
        first_x(h)
        now(h, 0)
        now(h, 1)
        for yo in range(4):
            emit(h, yo, 1, range(FY // 128, 4))
        for j in range(2):
            emit(h, 3, j, range(FY // 128))

    def final(h):
        for b in range(2):
            _, rows, _ = half(0, b)
            arrive(rx.at[h, rows], x_recv.at[h, b])
            part[h, 3, 1, rows] = part[h, 3, 1, rows] + rx[h, rows]
        for u in range(4):
            rr = pl.ds(u * 128, 128)
            v = part[h, 3, 1, rr]
            hi = v.astype(BF16)
            lo = (v - hi.astype(F32)).astype(BF16)
            m = (jnp.dot(hi, wb[h, 0], preferred_element_type=F32)
                 + jnp.dot(lo, wb[h, 0], preferred_element_type=F32)
                 + jnp.dot(hi, wb[h, 1], preferred_element_type=F32))
            ra, rb = pl.ds(u * 128, 128), pl.ds((u + 4) * 128, 128)
            if h == 0:
                out[ra, :] = m[:, :128]
                out[rb, :] = m[:, 128:]
            else:
                out[ra, :] = jnp.maximum(out[ra, :] + m[:, :128], 0.0)
                out[rb, :] = jnp.maximum(out[rb, :] + m[:, 128:], 0.0)

    barrier = pltpu.get_barrier_semaphore()
    around = (ZP, ZM, XP, SB, YP, YM, XL)
    for t in around:
        pl.semaphore_signal(barrier, inc=1, device_id=t, device_id_type=MESH)
    for p in range(ASTAGE):
        a_copy(p).start()

    for u in range(NB):
        for o in (u, u + 4):
            def take(i, _):
                for k in range(16):
                    at = o * 128 + i * 16 + k
                    ordered[pl.ds(at, 1), :] = feat[pl.ds(order[0, at], 1), :]
                return 0
            lax.fori_loop(0, 8, take, 0)
        pack(0, u)
    pl.semaphore_wait(barrier, len(around))
    start(0)
    more(0)
    ivec[...] = jnp.zeros_like(ivec)
    fvec[...] = jnp.zeros_like(fvec)
    tables()
    for copy in table_copies():
        copy.start()

    todo = iter(range(T // APIECE))

    def a_pieces(n):
        for _ in range(n):
            p = next(todo, None)
            if p is not None:
                a_piece(p)

    a_pieces(1)
    relay(0, 0)
    a_pieces(1)
    relay(0, 2)
    fill(0, 0)
    a_pieces(1)
    across(0, 0)
    fill(0, 2)
    a_pieces(1)
    across(0, 1)
    a_pieces(1)
    for b in range(NB):
        stage2(0, b)
        a_pieces(1)
    across(0, 2)
    a_pieces(1)
    across(0, 3)
    a_pieces(1)
    for u in range(4):
        pack(1, u)
    for h in range(2):
        convert(h, OWN)
    wb[...] = jnp.zeros_like(wb)
    for h in range(2):
        w = weight[pl.ds(h * 64, 64), :]
        hi = w.astype(BF16)
        for k, v in enumerate((hi, (w - hi.astype(F32)).astype(BF16))):
            wb[h, k, 0:64, 0:128] = v
            wb[h, k, 64:128, 128:256] = v
    for b in (0, 2):
        rest(0, b)
        a_pieces(1)
    for s in (P0, AM, AP, A2):
        convert(0, s)
        a_pieces(1)
    start(1)
    for b in range(NB):
        stage2b(0, b)
        a_pieces(1)
    more(1)
    a_pieces(T // APIECE)
    for s in (BM, BP):
        convert(0, s)
    for b in range(NB):
        stage3(0, b)
    convert(0, B2)
    for copy in table_copies():
        copy.wait()
    stage4(0)

    def both(*runs):
        def go():
            for f, *args in runs:
                f(*args)
        return go

    compute(0, {
        0: both((relay, 1, 0)),
        1: both((relay, 1, 2), (fill, 1, 0), (across, 1, 0), (fill, 1, 2)),
        2: both((across, 1, 1), (stage2, 1, 0), (stage2, 1, 1)),
        3: both((stage2, 1, 2), (stage2, 1, 3), (across, 1, 2), (rest, 1, 0)),
        4: both((across, 1, 3), (rest, 1, 2)),
    })
    sums_start(0)
    for s in (P0, AM, AP, A2):
        convert(1, s)
    for b in range(NB):
        stage2b(1, b)
    for s in (BM, BP):
        convert(1, s)
    for b in range(NB):
        stage3(1, b)
    convert(1, B2)
    stage4(1)

    compute(1, {
        0: both((adj_late, 0, 0), (first_add, 0)),
        1: both((adj_late, 0, 1)),
        2: both((adj_late, 0, 2)),
        4: both((own_sum, 0, 0)),
    })
    sums_start(1)
    adj_late(1, 0)
    own_sum(0, 1)
    first_add(1)
    adj_late(1, 1)
    own_sum(0, 2)
    final(0)
    own_sum(1, 0)
    adj_late(1, 2)
    own_sum(1, 1)
    own_sum(1, 2)
    final(1)
    for h in range(2):
        sent(recv.at[0, pl.ds(0, 15)], s_send.at[h])
        sent(recv.at[0, pl.ds(0, 7)], s_send.at[2 + h])


def shards(features, weight, adjacency_tiles, tile_rows, tile_cols, tile_counts, cluster_order):
    c = lax.axis_index("rep")
    y, xl = c // 2, c % 2
    j = jnp.arange(T, dtype=jnp.int32)
    dy, rx_, t = (tile_rows // 16 - y) % 4, (tile_rows // 8) % 2, tile_rows % 8
    yo = jnp.where(dy == 0, 3, jnp.where(dy == 1, 1, jnp.where(dy == 2, 0, 2)))
    rel = ((yo * 2 + (rx_ == xl)) * 4 + t % 4) * 2 + t // 4
    key = jnp.where(j < tile_counts[0], rel, 64)
    k, o = tile_cols // 8, tile_cols % 8
    panel = ((k % 2) * 8 + k // 2) * 4 + o % 4
    code = key * 65536 + (o // 4) * 32768 + panel * 512 + j
    more = jnp.arange(T, 384, dtype=jnp.int32) + 64 * 65536
    code = jnp.concatenate([code, more]).reshape(3, 128)
    smem = pl.BlockSpec(memory_space=pltpu.SMEM)
    vmem = pl.BlockSpec(memory_space=pltpu.VMEM)
    dma = pltpu.SemaphoreType.DMA
    return pl.pallas_call(
        body,
        out_shape=jax.ShapeDtypeStruct((1024, 128), F32),
        in_specs=[smem, vmem, vmem, vmem, pl.BlockSpec(memory_space=pl.ANY)],
        out_specs=vmem,
        scratch_shapes=[
            pltpu.VMEM((2, 16, 512, 128), F32),
            pltpu.VMEM((2, 64, 128, 256), BF16),
            pltpu.VMEM((T, 128, 256), BF16),
            pltpu.VMEM((ASTAGE, APIECE, 128, 128), F32),
            pltpu.VMEM((T // 2, 128, 128), F32),
            pltpu.VMEM((2, 4, 2, 512, 128), F32),
            pltpu.VMEM((2, 4, 512 - FY, 128), F32),
            pltpu.VMEM((2, 2, 3, FY // 2, 128), F32),
            pltpu.VMEM((2, 2, 2, 512, 128), F32),
            pltpu.VMEM((2, 512, 128), F32),
            pltpu.VMEM((1024, 128), F32),
            pltpu.VMEM((2, 2, 128, 256), BF16),
            pltpu.VMEM((16, 128), jnp.int32),
            pltpu.VMEM((16, 128), F32),
            pltpu.SMEM((16, 128), jnp.int32),
            pltpu.SMEM((16, 128), F32),
            dma((2, 8, NB)),
            dma((2, 8)),
            dma((4,)),
            dma((2,)),
            dma((2, 2, 3)),
            dma((2, 2, 3, 2)),
            dma((2, 2)),
            dma((ASTAGE,)),
            dma((2,)),
        ],
        compiler_params=pltpu.CompilerParams(
            collective_id=0, has_side_effects=True, vmem_limit_bytes=63 * 1024 * 1024),
    )(cluster_order, code, features, weight, adjacency_tiles)


def solution(mesh):
    placed = (
        P(("row", "rep"), None),
        P(),
        P(("row", "rep"), None, None),
        P(("row", "rep")),
        P(("row", "rep")),
        P(("row", "rep")),
        P(("row", "rep"), None),
    )
    return jax.shard_map(
        shards, mesh=mesh, in_specs=placed, out_specs=P(("row", "rep"), None), check_vma=False
    )
```

```python
import functools

import jax
import jax.numpy as jnp
from jax import lax
from jax.experimental import pallas as pl
from jax.experimental.pallas import tpu as pltpu
from jax.sharding import PartitionSpec as P

MESH = pl.DeviceIdType.MESH
F32, BF16 = jnp.float32, jnp.bfloat16
T = 320
NB = 4
APIECE = 16
ASTAGE = 4
UNROLL = 64
FY = 384


def body(order, code, feat, weight, adj, out,
         recv, panels, aq, astage, cbuf, part, first, ropp, radj, rx, ordered, wb,
         ivec, fvec, itab, ftab, g_recv, c_recv, s_send, f_recv, o_recv, a_recv, x_recv, a_sem, t_sem):
    r, c = lax.axis_index("row"), lax.axis_index("rep")
    z, xh, kp = r // 4, (r // 2) % 2, r % 2
    y, xl = c // 2, c % 2
    zp, zm, z2 = (z + 1) % 4, (z + 3) % 4, (z + 2) % 4

    ZP = (zp * 4 + xh * 2 + kp, c)
    ZM = (zm * 4 + xh * 2 + kp, c)
    XP = (z * 4 + (1 - xh) * 2 + kp, c)
    SB = (z * 4 + xh * 2 + (1 - kp), c)
    YP = (r, ((y + 1) % 4) * 2 + xl)
    YM = (r, ((y + 3) % 4) * 2 + xl)
    XL = (r, y * 2 + (1 - xl))

    def slot(zz, xx, kk):
        return kk * 8 + zz * 2 + xx

    OWN, P0 = slot(z, xh, kp), slot(z, 1 - xh, kp)
    AP, AM, A2 = slot(zp, xh, kp), slot(zm, xh, kp), slot(z2, xh, kp)
    BP, BM, B2 = slot(zp, 1 - xh, kp), slot(zm, 1 - xh, kp), slot(z2, 1 - xh, kp)

    lane = lax.broadcasted_iota(jnp.int32, (128, 128), 1) < 64
    def remote(src, dst, ssem, rsem, target):
        pltpu.make_async_remote_copy(
            src_ref=src, dst_ref=dst, send_sem=ssem, recv_sem=rsem,
            device_id=target, device_id_type=MESH).start()

    def arrive(ref, rsem):
        pltpu.make_async_remote_copy(
            src_ref=ref, dst_ref=ref, send_sem=s_send.at[0], recv_sem=rsem,
            device_id=SB, device_id_type=MESH).wait_recv()

    def sent(ref, ssem):
        pltpu.make_async_remote_copy(
            src_ref=ref, dst_ref=ref, send_sem=ssem, recv_sem=f_recv.at[0],
            device_id=SB, device_id_type=MESH).wait_send()

    def piece(h, s, b):
        return recv.at[h, s, pl.ds(b * 128, 128)]

    def give(h, s, b, *targets):
        for t in targets:
            there = c_recv.at[h, s % 8] if t is SB else g_recv.at[h, s % 8, b]
            remote(piece(h, s, b), piece(h, s, b), s_send.at[h], there, t)

    def got(h, s, b):
        arrive(piece(h, s, b), g_recv.at[h, s % 8, b])

    def convert(h, s):
        def unit(u, _):
            v = recv[h, s, pl.ds(pl.multiple_of(u * 128, 128), 128), :]
            hi = v.astype(BF16)
            panels[h, s * 4 + u, :, 0:128] = hi
            panels[h, s * 4 + u, :, 128:256] = (v - hi.astype(F32)).astype(BF16)
            return 0
        lax.fori_loop(0, 4, unit, 0, unroll=2)

    def pack(h, u):
        a = ordered[pl.ds(u * 128, 128), :]
        b = ordered[pl.ds((u + 4) * 128, 128), :]
        if h == 0:
            v = jnp.where(lane, a, pltpu.roll(b, 64, 1))
        else:
            v = jnp.where(lane, pltpu.roll(a, 64, 1), b)
        recv[h, OWN, pl.ds(u * 128, 128), :] = v

    def start(h):
        for b in (0, 2):
            give(h, OWN, b, ZP)
            give(h, OWN, b + 1, ZM)
        for b in (0, 1):
            give(h, OWN, b, XP)

    def more(h):
        for b in (2, 3):
            give(h, OWN, b, XP)
        for b in range(NB):
            give(h, OWN, b, SB)

    def fill(h, b):
        give(h, OWN, b + 1, ZP)
        give(h, OWN, b, ZM)

    def relay(h, b):
        got(h, AM, b)
        give(h, AM, b, ZP, SB)
        got(h, AP, b + 1)
        give(h, AP, b + 1, ZM, SB)

    def across(h, b):
        got(h, P0, b)
        give(h, P0, b, ZP, ZM, SB)

    def rest(h, b):
        got(h, AM, b + 1)
        give(h, AM, b + 1, SB)
        got(h, AP, b)
        give(h, AP, b, SB)

    def stage2(h, b):
        got(h, A2, b)
        give(h, A2, b, XP, SB)

    def stage2b(h, b):
        got(h, BM, b)
        give(h, BM, b, SB)
        got(h, BP, b)
        give(h, BP, b, SB)

    def stage3(h, b):
        got(h, B2, b)
        give(h, B2, b, SB)

    def stage4(h):
        k = 1 - kp
        for s in (slot(z, xh, k), slot(z, 1 - xh, k), slot(zp, xh, k), slot(zm, xh, k),
                  slot(z2, xh, k), slot(zp, 1 - xh, k), slot(zm, 1 - xh, k), slot(z2, 1 - xh, k)):
            arrive(recv.at[h, s], c_recv.at[h, s % 8])
            convert(h, s)

    def a_copy(p):
        return pltpu.make_async_copy(
            adj.at[pl.ds(p * APIECE, APIECE)], astage.at[p % ASTAGE], a_sem.at[p % ASTAGE])

    def a_piece(p):
        a_copy(p).wait()

        def tile(t, _):
            v = astage[p % ASTAGE, t]
            hi = v.astype(BF16)
            aq[p * APIECE + t, :, 0:128] = hi
            aq[p * APIECE + t, :, 128:256] = (v - hi.astype(F32)).astype(BF16)
            return 0
        lax.fori_loop(0, APIECE, tile, 0, unroll=2)
        if p + ASTAGE < T // APIECE:
            a_copy(p + ASTAGE).start()

    def compute(h, events):
        low = lax.broadcasted_iota(jnp.int32, (1, 128), 1) < 64

        def step(i, acc):
            row, col = i // (128 // UNROLL), (i % (128 // UNROLL)) * UNROLL

            def add(u, acc):
                w = panels[h, itab[3 + row, col + u]]
                p = jnp.dot(aq[itab[row, col + u]], jnp.concatenate([w, w], 0),
                            preferred_element_type=F32)
                side = jnp.where(low, ftab[3 + row, col + u], ftab[6 + row, col + u])
                return acc * ftab[row, col + u] + (p[:, :128] + p[:, 128:]) * side

            for u in range(0, UNROLL, 2):
                a0 = add(u, acc)
                acc = add(u + 1, a0)
                cbuf[i * (UNROLL // 2) + u // 2] = jnp.where(lane, a0, acc) + pltpu.roll(
                    jnp.where(lane, acc, a0), 64, 1)
            for k, run in events.items():
                pl.when(i == k)(run)
            return acc
        lax.fori_loop(0, T // UNROLL, step, jnp.zeros((128, 128), F32))

    def emit(h, yo, j, units=range(4)):
        low = lax.broadcasted_iota(jnp.int32, (1, 128), 1) < 64
        for u in units:
            e = ((yo * 2 + j) * 4 + u) * 2
            v, w = cbuf[itab[6, e]], cbuf[itab[6, e + 1]]
            stay = jnp.where(low, ftab[9, e], ftab[10, e + 1])
            turn = jnp.where(low, ftab[10, e], ftab[9, e + 1])
            part[h, yo, j, pl.ds(u * 128, 128), :] = (
                jnp.where(lane, v, w) * stay + pltpu.roll(jnp.where(lane, w, v), 64, 1) * turn)

    def tables():
        def down(v):
            return jnp.transpose(jnp.broadcast_to(v, (128, 128)))

        def total(v):
            return jnp.sum(v, axis=0, keepdims=True)
        at = lax.broadcasted_iota(jnp.int32, (1, 128), 1)
        rows = [code[pl.ds(k, 1), :] for k in range(3)]
        cols = [down(v) for v in rows]
        ranks = [down(sum(total((m < v).astype(jnp.int32)) for m in cols)) for v in rows]
        for k in range(3):
            here = sum(total(jnp.where(n == at + k * 128, m, 0)) for n, m in zip(ranks, cols))
            back = sum(total(jnp.where(n == at + (k * 128 - 1), m, 0)) for n, m in zip(ranks, cols))
            side = (here // 32768) % 2
            ivec[pl.ds(k, 1), :] = jnp.minimum(here % 512, T - 1)
            ivec[pl.ds(3 + k, 1), :] = (here // 512) % 64
            fvec[pl.ds(k, 1), :] = (here // 65536 == back // 65536).astype(F32)
            fvec[pl.ds(3 + k, 1), :] = (1 - side).astype(F32)
            fvec[pl.ds(6 + k, 1), :] = side.astype(F32)
        upto = sum(total((m // 65536 <= at).astype(jnp.int32)) for m in cols)
        before = sum(total((m // 65536 < at).astype(jnp.int32)) for m in cols)
        last = jnp.clip(upto - 1, 0, T - 1)
        has = jnp.where(upto > before, 1, 0)
        ivec[pl.ds(6, 1), :] = last // 2
        fvec[pl.ds(9, 1), :] = (has * (1 - last % 2)).astype(F32)
        fvec[pl.ds(10, 1), :] = (has * (last % 2)).astype(F32)

    def table_copies():
        return (pltpu.make_async_copy(ivec, itab, t_sem.at[0]),
                pltpu.make_async_copy(fvec, ftab, t_sem.at[1]))

    LATE = pl.ds(FY, 512 - FY)

    def half(j, b):
        n = FY // 2 if j < 2 else (512 - FY) // 2
        return min(j, 1), pl.ds((FY if j == 2 else 0) + b * n, n), pl.ds(0, n)

    def first_x(h):
        remote(part.at[h, :, 0, LATE], first.at[h], s_send.at[2 + h], f_recv.at[h], XL)

    def first_add(h):
        arrive(first.at[h], f_recv.at[h])
        for yo in range(4):
            part[h, yo, 1, LATE] = part[h, yo, 1, LATE] + first[h, yo]
        now(h, 2)

    def adj_send(h, j, d, b):
        k, rows, _ = half(j, b)
        remote(part.at[h, 1 + d, k, rows], radj.at[h, d, k, rows],
               s_send.at[2 + h], a_recv.at[h, d, j, b], (YP, YM)[d])

    def now(h, j):
        for d in range(2):
            k, rows, there = half(j, d)
            if j < 2:
                emit(h, 0, k, range(0 if d == 0 else 2, 2 if d == 0 else 3))
            remote(part.at[h, 0, k, rows], ropp.at[h, d, j, there],
                   s_send.at[2 + h], o_recv.at[h, d, j], (YP, YM)[d])
        for d in range(2):
            if j < 2:
                emit(h, 1 + d, k, range(FY // 128))
            adj_send(h, j, d, 1 - d)

    def adj_late(h, j):
        for d in range(2):
            k, rows, there = half(j, d)
            arrive(ropp.at[h, d, j, there], o_recv.at[h, d, j])
            part[h, 1 + d, k, rows] = part[h, 1 + d, k, rows] + ropp[h, d, j, there]
            adj_send(h, j, d, d)

    def own_sum(h, j):
        for b in (1, 0):
            k, rows, _ = half(j, b)
            for d in range(2):
                arrive(radj.at[h, d, k, rows], a_recv.at[h, d, j, b])
            part[h, 3, k, rows] = part[h, 3, k, rows] + (radj[h, 0, k, rows] + radj[h, 1, k, rows])
            if j == 0:
                remote(part.at[h, 3, 0, rows], rx.at[h, rows], s_send.at[2 + h], x_recv.at[h, b], XL)

    def sums_start(h):
        for yo in range(4):
            emit(h, yo, 0, range(FY // 128, 4))
        if h == 1:
            first_x(h)
        now(h, 0)
        now(h, 1)
        for yo in range(4):
            emit(h, yo, 1, range(FY // 128, 4))
        for j in range(2):
            emit(h, 3, j, range(FY // 128))

    def final(h):
        for b in range(2):
            _, rows, _ = half(0, b)
            arrive(rx.at[h, rows], x_recv.at[h, b])
            part[h, 3, 1, rows] = part[h, 3, 1, rows] + rx[h, rows]
        for u in range(4):
            rr = pl.ds(u * 128, 128)
            v = part[h, 3, 1, rr]
            hi = v.astype(BF16)
            lo = (v - hi.astype(F32)).astype(BF16)
            m = (jnp.dot(hi, wb[h, 0], preferred_element_type=F32)
                 + jnp.dot(lo, wb[h, 0], preferred_element_type=F32)
                 + jnp.dot(hi, wb[h, 1], preferred_element_type=F32))
            ra, rb = pl.ds(u * 128, 128), pl.ds((u + 4) * 128, 128)
            if h == 0:
                out[ra, :] = m[:, :128]
                out[rb, :] = m[:, 128:]
            else:
                out[ra, :] = jnp.maximum(out[ra, :] + m[:, :128], 0.0)
                out[rb, :] = jnp.maximum(out[rb, :] + m[:, 128:], 0.0)

    barrier = pltpu.get_barrier_semaphore()
    around = (ZP, ZM, XP, SB, YP, YM, XL)
    for t in around:
        pl.semaphore_signal(barrier, inc=1, device_id=t, device_id_type=MESH)
    for p in range(ASTAGE):
        a_copy(p).start()

    for u in range(NB):
        for o in (u, u + 4):
            def take(i, _):
                for k in range(16):
                    at = o * 128 + i * 16 + k
                    ordered[pl.ds(at, 1), :] = feat[pl.ds(order[0, at], 1), :]
                return 0
            lax.fori_loop(0, 8, take, 0)
        pack(0, u)
    pl.semaphore_wait(barrier, len(around))
    start(0)
    more(0)
    ivec[...] = jnp.zeros_like(ivec)
    fvec[...] = jnp.zeros_like(fvec)
    tables()
    for copy in table_copies():
        copy.start()

    todo = iter(range(T // APIECE))

    def a_pieces(n):
        for _ in range(n):
            p = next(todo, None)
            if p is not None:
                a_piece(p)

    a_pieces(1)
    relay(0, 0)
    a_pieces(1)
    relay(0, 2)
    fill(0, 0)
    a_pieces(1)
    across(0, 0)
    fill(0, 2)
    a_pieces(1)
    across(0, 1)
    a_pieces(1)
    for b in range(NB):
        stage2(0, b)
        a_pieces(1)
    across(0, 2)
    a_pieces(1)
    across(0, 3)
    a_pieces(1)
    for u in range(4):
        pack(1, u)
    for h in range(2):
        convert(h, OWN)
    wb[...] = jnp.zeros_like(wb)
    for h in range(2):
        w = weight[pl.ds(h * 64, 64), :]
        hi = w.astype(BF16)
        for k, v in enumerate((hi, (w - hi.astype(F32)).astype(BF16))):
            wb[h, k, 0:64, 0:128] = v
            wb[h, k, 64:128, 128:256] = v
    for b in (0, 2):
        rest(0, b)
        a_pieces(1)
    for s in (P0, AM, AP, A2):
        convert(0, s)
        a_pieces(1)
    start(1)
    for b in range(NB):
        stage2b(0, b)
        a_pieces(1)
    more(1)
    a_pieces(T // APIECE)
    for s in (BM, BP):
        convert(0, s)
    for b in range(NB):
        stage3(0, b)
    convert(0, B2)
    for copy in table_copies():
        copy.wait()
    fill(1, 0)
    stage4(0)

    def both(*runs):
        def go():
            for f, *args in runs:
                f(*args)
        return go

    compute(0, {
        0: both((relay, 1, 0), (relay, 1, 2)),
        1: both((fill, 1, 2), (across, 1, 0)),
        2: both((across, 1, 1), (stage2, 1, 0), (stage2, 1, 1)),
        3: both((stage2, 1, 2), (stage2, 1, 3), (across, 1, 2), (rest, 1, 0)),
        4: both((across, 1, 3), (rest, 1, 2)),
    })
    sums_start(0)
    for s in (P0, AM, AP, A2):
        convert(1, s)
    for b in range(NB):
        stage2b(1, b)
    for b in range(NB):
        stage3(1, b)
    first_x(0)
    for s in (BM, BP):
        convert(1, s)
    convert(1, B2)
    stage4(1)

    compute(1, {
        0: both((adj_late, 0, 0)),
        1: both((adj_late, 0, 1)),
        2: both((first_add, 0)),
        3: both((own_sum, 0, 0)),
        4: both((adj_late, 0, 2)),
    })
    sums_start(1)
    adj_late(1, 0)
    own_sum(0, 1)
    first_add(1)
    adj_late(1, 1)
    own_sum(0, 2)
    final(0)
    own_sum(1, 0)
    adj_late(1, 2)
    own_sum(1, 1)
    own_sum(1, 2)
    final(1)
    for h in range(2):
        sent(recv.at[0, pl.ds(0, 15)], s_send.at[h])
        sent(recv.at[0, pl.ds(0, 7)], s_send.at[2 + h])


def shards(features, weight, adjacency_tiles, tile_rows, tile_cols, tile_counts, cluster_order):
    c = lax.axis_index("rep")
    y, xl = c // 2, c % 2
    j = jnp.arange(T, dtype=jnp.int32)
    dy, rx_, t = (tile_rows // 16 - y) % 4, (tile_rows // 8) % 2, tile_rows % 8
    yo = jnp.where(dy == 0, 3, jnp.where(dy == 1, 1, jnp.where(dy == 2, 0, 2)))
    rel = ((yo * 2 + (rx_ == xl)) * 4 + t % 4) * 2 + t // 4
    key = jnp.where(j < tile_counts[0], rel, 64)
    k, o = tile_cols // 8, tile_cols % 8
    panel = ((k % 2) * 8 + k // 2) * 4 + o % 4
    code = key * 65536 + (o // 4) * 32768 + panel * 512 + j
    more = jnp.arange(T, 384, dtype=jnp.int32) + 64 * 65536
    code = jnp.concatenate([code, more]).reshape(3, 128)
    smem = pl.BlockSpec(memory_space=pltpu.SMEM)
    vmem = pl.BlockSpec(memory_space=pltpu.VMEM)
    dma = pltpu.SemaphoreType.DMA
    return pl.pallas_call(
        body,
        out_shape=jax.ShapeDtypeStruct((1024, 128), F32),
        in_specs=[smem, vmem, vmem, vmem, pl.BlockSpec(memory_space=pl.ANY)],
        out_specs=vmem,
        scratch_shapes=[
            pltpu.VMEM((2, 16, 512, 128), F32),
            pltpu.VMEM((2, 64, 128, 256), BF16),
            pltpu.VMEM((T, 128, 256), BF16),
            pltpu.VMEM((ASTAGE, APIECE, 128, 128), F32),
            pltpu.VMEM((T // 2, 128, 128), F32),
            pltpu.VMEM((2, 4, 2, 512, 128), F32),
            pltpu.VMEM((2, 4, 512 - FY, 128), F32),
            pltpu.VMEM((2, 2, 3, FY // 2, 128), F32),
            pltpu.VMEM((2, 2, 2, 512, 128), F32),
            pltpu.VMEM((2, 512, 128), F32),
            pltpu.VMEM((1024, 128), F32),
            pltpu.VMEM((2, 2, 128, 256), BF16),
            pltpu.VMEM((16, 128), jnp.int32),
            pltpu.VMEM((16, 128), F32),
            pltpu.SMEM((16, 128), jnp.int32),
            pltpu.SMEM((16, 128), F32),
            dma((2, 8, NB)),
            dma((2, 8)),
            dma((4,)),
            dma((2,)),
            dma((2, 2, 3)),
            dma((2, 2, 3, 2)),
            dma((2, 2)),
            dma((ASTAGE,)),
            dma((2,)),
        ],
        compiler_params=pltpu.CompilerParams(
            collective_id=0, has_side_effects=True, vmem_limit_bytes=63 * 1024 * 1024),
    )(cluster_order, code, features, weight, adjacency_tiles)


def solution(mesh):
    placed = (
        P(("row", "rep"), None),
        P(),
        P(("row", "rep"), None, None),
        P(("row", "rep")),
        P(("row", "rep")),
        P(("row", "rep")),
        P(("row", "rep"), None),
    )
    return jax.shard_map(
        shards, mesh=mesh, in_specs=placed, out_specs=P(("row", "rep"), None), check_vma=False
    )
```

```python
import functools

import jax
import jax.numpy as jnp
from jax import lax
from jax.experimental import pallas as pl
from jax.experimental.pallas import tpu as pltpu
from jax.sharding import PartitionSpec as P

MESH = pl.DeviceIdType.MESH
F32, BF16 = jnp.float32, jnp.bfloat16
T = 320
NB = 4
APIECE = 16
ASTAGE = 4
UNROLL = 64
FY = 384


def body(order, code, feat, weight, adj, out,
         recv, panels, aq, astage, cbuf, part, first, ropp, radj, rx, ordered, wb,
         ivec, fvec, itab, ftab, g_recv, c_recv, s_send, f_recv, o_recv, a_recv, x_recv, a_sem, t_sem):
    r, c = lax.axis_index("row"), lax.axis_index("rep")
    z, xh, kp = r // 4, (r // 2) % 2, r % 2
    y, xl = c // 2, c % 2
    zp, zm, z2 = (z + 1) % 4, (z + 3) % 4, (z + 2) % 4

    ZP = (zp * 4 + xh * 2 + kp, c)
    ZM = (zm * 4 + xh * 2 + kp, c)
    XP = (z * 4 + (1 - xh) * 2 + kp, c)
    SB = (z * 4 + xh * 2 + (1 - kp), c)
    YP = (r, ((y + 1) % 4) * 2 + xl)
    YM = (r, ((y + 3) % 4) * 2 + xl)
    XL = (r, y * 2 + (1 - xl))

    def slot(zz, xx, kk):
        return kk * 8 + zz * 2 + xx

    OWN, P0 = slot(z, xh, kp), slot(z, 1 - xh, kp)
    AP, AM, A2 = slot(zp, xh, kp), slot(zm, xh, kp), slot(z2, xh, kp)
    BP, BM, B2 = slot(zp, 1 - xh, kp), slot(zm, 1 - xh, kp), slot(z2, 1 - xh, kp)

    lane = lax.broadcasted_iota(jnp.int32, (128, 128), 1) < 64
    def remote(src, dst, ssem, rsem, target):
        pltpu.make_async_remote_copy(
            src_ref=src, dst_ref=dst, send_sem=ssem, recv_sem=rsem,
            device_id=target, device_id_type=MESH).start()

    def arrive(ref, rsem):
        pltpu.make_async_remote_copy(
            src_ref=ref, dst_ref=ref, send_sem=s_send.at[0], recv_sem=rsem,
            device_id=SB, device_id_type=MESH).wait_recv()

    def sent(ref, ssem):
        pltpu.make_async_remote_copy(
            src_ref=ref, dst_ref=ref, send_sem=ssem, recv_sem=f_recv.at[0],
            device_id=SB, device_id_type=MESH).wait_send()

    def piece(h, s, b):
        return recv.at[h, s, pl.ds(b * 128, 128)]

    def give(h, s, b, *targets):
        for t in targets:
            there = c_recv.at[h, s % 8] if t is SB else g_recv.at[h, s % 8, b]
            remote(piece(h, s, b), piece(h, s, b), s_send.at[h], there, t)

    def got(h, s, b):
        arrive(piece(h, s, b), g_recv.at[h, s % 8, b])

    def convert(h, s):
        def unit(u, _):
            v = recv[h, s, pl.ds(pl.multiple_of(u * 128, 128), 128), :]
            hi = v.astype(BF16)
            panels[h, s * 4 + u, :, 0:128] = hi
            panels[h, s * 4 + u, :, 128:256] = (v - hi.astype(F32)).astype(BF16)
            return 0
        lax.fori_loop(0, 4, unit, 0, unroll=2)

    def pack(h, u):
        a = ordered[pl.ds(u * 128, 128), :]
        b = ordered[pl.ds((u + 4) * 128, 128), :]
        if h == 0:
            v = jnp.where(lane, a, pltpu.roll(b, 64, 1))
        else:
            v = jnp.where(lane, pltpu.roll(a, 64, 1), b)
        recv[h, OWN, pl.ds(u * 128, 128), :] = v

    def start(h):
        for b in (0, 2):
            give(h, OWN, b, ZP)
            give(h, OWN, b + 1, ZM)
        for b in (0, 1):
            give(h, OWN, b, XP)

    def more(h):
        for b in (2, 3):
            give(h, OWN, b, XP)
        for b in range(NB):
            give(h, OWN, b, SB)

    def fill(h, b):
        give(h, OWN, b + 1, ZP)
        give(h, OWN, b, ZM)

    def relay(h, b):
        got(h, AM, b)
        give(h, AM, b, ZP, SB)
        got(h, AP, b + 1)
        give(h, AP, b + 1, ZM, SB)

    def across(h, b):
        got(h, P0, b)
        give(h, P0, b, ZP, ZM, SB)

    def rest(h, b):
        got(h, AM, b + 1)
        give(h, AM, b + 1, SB)
        got(h, AP, b)
        give(h, AP, b, SB)

    def stage2(h, b):
        got(h, A2, b)
        give(h, A2, b, XP, SB)

    def stage2b(h, b):
        got(h, BM, b)
        give(h, BM, b, SB)
        got(h, BP, b)
        give(h, BP, b, SB)

    def stage3(h, b):
        got(h, B2, b)
        give(h, B2, b, SB)

    def stage4(h):
        k = 1 - kp
        for s in (slot(z, xh, k), slot(z, 1 - xh, k), slot(zp, xh, k), slot(zm, xh, k),
                  slot(z2, xh, k), slot(zp, 1 - xh, k), slot(zm, 1 - xh, k), slot(z2, 1 - xh, k)):
            arrive(recv.at[h, s], c_recv.at[h, s % 8])
            convert(h, s)

    def a_copy(p):
        return pltpu.make_async_copy(
            adj.at[pl.ds(p * APIECE, APIECE)], astage.at[p % ASTAGE], a_sem.at[p % ASTAGE])

    def a_piece(p):
        a_copy(p).wait()

        def tile(t, _):
            v = astage[p % ASTAGE, t]
            hi = v.astype(BF16)
            aq[p * APIECE + t, :, 0:128] = hi
            aq[p * APIECE + t, :, 128:256] = (v - hi.astype(F32)).astype(BF16)
            return 0
        lax.fori_loop(0, APIECE, tile, 0, unroll=2)
        if p + ASTAGE < T // APIECE:
            a_copy(p + ASTAGE).start()

    def compute(h, events):
        low = lax.broadcasted_iota(jnp.int32, (1, 128), 1) < 64

        def step(i, acc):
            row, col = i // (128 // UNROLL), (i % (128 // UNROLL)) * UNROLL

            def add(u, acc):
                w = panels[h, itab[3 + row, col + u]]
                p = jnp.dot(aq[itab[row, col + u]], jnp.concatenate([w, w], 0),
                            preferred_element_type=F32)
                side = jnp.where(low, ftab[3 + row, col + u], ftab[6 + row, col + u])
                return acc * ftab[row, col + u] + (p[:, :128] + p[:, 128:]) * side

            for u in range(0, UNROLL, 2):
                a0 = add(u, acc)
                acc = add(u + 1, a0)
                cbuf[i * (UNROLL // 2) + u // 2] = jnp.where(lane, a0, acc) + pltpu.roll(
                    jnp.where(lane, acc, a0), 64, 1)
            for k, run in events.items():
                pl.when(i == k)(run)
            return acc
        lax.fori_loop(0, T // UNROLL, step, jnp.zeros((128, 128), F32))

    def emit(h, yo, j, units=range(4)):
        low = lax.broadcasted_iota(jnp.int32, (1, 128), 1) < 64
        for u in units:
            e = ((yo * 2 + j) * 4 + u) * 2
            v, w = cbuf[itab[6, e]], cbuf[itab[6, e + 1]]
            stay = jnp.where(low, ftab[9, e], ftab[10, e + 1])
            turn = jnp.where(low, ftab[10, e], ftab[9, e + 1])
            part[h, yo, j, pl.ds(u * 128, 128), :] = (
                jnp.where(lane, v, w) * stay + pltpu.roll(jnp.where(lane, w, v), 64, 1) * turn)

    def tables():
        def down(v):
            return jnp.transpose(jnp.broadcast_to(v, (128, 128)))

        def total(v):
            return jnp.sum(v, axis=0, keepdims=True)
        at = lax.broadcasted_iota(jnp.int32, (1, 128), 1)
        rows = [code[pl.ds(k, 1), :] for k in range(3)]
        cols = [down(v) for v in rows]
        ranks = [down(sum(total((m < v).astype(jnp.int32)) for m in cols)) for v in rows]
        for k in range(3):
            here = sum(total(jnp.where(n == at + k * 128, m, 0)) for n, m in zip(ranks, cols))
            back = sum(total(jnp.where(n == at + (k * 128 - 1), m, 0)) for n, m in zip(ranks, cols))
            side = (here // 32768) % 2
            ivec[pl.ds(k, 1), :] = jnp.minimum(here % 512, T - 1)
            ivec[pl.ds(3 + k, 1), :] = (here // 512) % 64
            fvec[pl.ds(k, 1), :] = (here // 65536 == back // 65536).astype(F32)
            fvec[pl.ds(3 + k, 1), :] = (1 - side).astype(F32)
            fvec[pl.ds(6 + k, 1), :] = side.astype(F32)
        upto = sum(total((m // 65536 <= at).astype(jnp.int32)) for m in cols)
        before = sum(total((m // 65536 < at).astype(jnp.int32)) for m in cols)
        last = jnp.clip(upto - 1, 0, T - 1)
        has = jnp.where(upto > before, 1, 0)
        ivec[pl.ds(6, 1), :] = last // 2
        fvec[pl.ds(9, 1), :] = (has * (1 - last % 2)).astype(F32)
        fvec[pl.ds(10, 1), :] = (has * (last % 2)).astype(F32)

    def table_copies():
        return (pltpu.make_async_copy(ivec, itab, t_sem.at[0]),
                pltpu.make_async_copy(fvec, ftab, t_sem.at[1]))

    LATE = pl.ds(FY, 512 - FY)

    def half(j, b):
        n = FY // 2 if j < 2 else (512 - FY) // 2
        return min(j, 1), pl.ds((FY if j == 2 else 0) + b * n, n), pl.ds(0, n)

    def first_x(h):
        remote(part.at[h, :, 0, LATE], first.at[h], s_send.at[2 + h], f_recv.at[h], XL)

    def first_add(h):
        arrive(first.at[h], f_recv.at[h])
        for yo in range(4):
            part[h, yo, 1, LATE] = part[h, yo, 1, LATE] + first[h, yo]
        now(h, 2)

    def adj_send(h, j, d, b):
        k, rows, _ = half(j, b)
        remote(part.at[h, 1 + d, k, rows], radj.at[h, d, k, rows],
               s_send.at[2 + h], a_recv.at[h, d, j, b], (YP, YM)[d])

    def now(h, j):
        for d in range(2):
            k, rows, there = half(j, d)
            if j < 2:
                emit(h, 0, k, range(0 if d == 0 else 2, 2 if d == 0 else 3))
            remote(part.at[h, 0, k, rows], ropp.at[h, d, j, there],
                   s_send.at[2 + h], o_recv.at[h, d, j], (YP, YM)[d])
        for d in range(2):
            if j < 2:
                emit(h, 1 + d, k, range(FY // 128))
            adj_send(h, j, d, 1 - d)

    def adj_late(h, j):
        for d in range(2):
            k, rows, there = half(j, d)
            arrive(ropp.at[h, d, j, there], o_recv.at[h, d, j])
            part[h, 1 + d, k, rows] = part[h, 1 + d, k, rows] + ropp[h, d, j, there]
            adj_send(h, j, d, d)

    def own_sum(h, j):
        for b in (1, 0):
            k, rows, _ = half(j, b)
            for d in range(2):
                arrive(radj.at[h, d, k, rows], a_recv.at[h, d, j, b])
            part[h, 3, k, rows] = part[h, 3, k, rows] + (radj[h, 0, k, rows] + radj[h, 1, k, rows])
            if j == 0:
                remote(part.at[h, 3, 0, rows], rx.at[h, rows], s_send.at[2 + h], x_recv.at[h, b], XL)

    def sums_start(h):
        for yo in range(4):
            emit(h, yo, 0, range(FY // 128, 4))
        if h == 1:
            first_x(h)
        now(h, 0)
        now(h, 1)
        for yo in range(4):
            emit(h, yo, 1, range(FY // 128, 4))
        for j in range(2):
            emit(h, 3, j, range(FY // 128))

    def final(h):
        for b in range(2):
            _, rows, _ = half(0, b)
            arrive(rx.at[h, rows], x_recv.at[h, b])
            part[h, 3, 1, rows] = part[h, 3, 1, rows] + rx[h, rows]
        for u in range(4):
            rr = pl.ds(u * 128, 128)
            v = part[h, 3, 1, rr]
            hi = v.astype(BF16)
            lo = (v - hi.astype(F32)).astype(BF16)
            m = (jnp.dot(hi, wb[h, 0], preferred_element_type=F32)
                 + jnp.dot(lo, wb[h, 0], preferred_element_type=F32)
                 + jnp.dot(hi, wb[h, 1], preferred_element_type=F32))
            ra, rb = pl.ds(u * 128, 128), pl.ds((u + 4) * 128, 128)
            if h == 0:
                out[ra, :] = m[:, :128]
                out[rb, :] = m[:, 128:]
            else:
                out[ra, :] = jnp.maximum(out[ra, :] + m[:, :128], 0.0)
                out[rb, :] = jnp.maximum(out[rb, :] + m[:, 128:], 0.0)

    barrier = pltpu.get_barrier_semaphore()
    around = (ZP, ZM, XP, SB, YP, YM, XL)
    for t in around:
        pl.semaphore_signal(barrier, inc=1, device_id=t, device_id_type=MESH)
    for p in range(ASTAGE):
        a_copy(p).start()

    for u in range(NB):
        for o in (u, u + 4):
            def take(i, _):
                for k in range(16):
                    at = o * 128 + i * 16 + k
                    ordered[pl.ds(at, 1), :] = feat[pl.ds(order[0, at], 1), :]
                return 0
            lax.fori_loop(0, 8, take, 0)
        pack(0, u)
    pl.semaphore_wait(barrier, len(around))
    start(0)
    fill(0, 0)
    more(0)
    ivec[...] = jnp.zeros_like(ivec)
    fvec[...] = jnp.zeros_like(fvec)
    tables()
    for copy in table_copies():
        copy.start()

    todo = iter(range(T // APIECE))

    def a_pieces(n):
        for _ in range(n):
            p = next(todo, None)
            if p is not None:
                a_piece(p)

    a_pieces(1)
    relay(0, 0)
    a_pieces(1)
    relay(0, 2)
    a_pieces(1)
    across(0, 0)
    fill(0, 2)
    a_pieces(1)
    across(0, 1)
    a_pieces(1)
    for b in range(NB):
        stage2(0, b)
        a_pieces(1)
    across(0, 2)
    a_pieces(1)
    across(0, 3)
    a_pieces(1)
    for u in range(4):
        pack(1, u)
    for h in range(2):
        convert(h, OWN)
    wb[...] = jnp.zeros_like(wb)
    for h in range(2):
        w = weight[pl.ds(h * 64, 64), :]
        hi = w.astype(BF16)
        for k, v in enumerate((hi, (w - hi.astype(F32)).astype(BF16))):
            wb[h, k, 0:64, 0:128] = v
            wb[h, k, 64:128, 128:256] = v
    for b in (0, 2):
        rest(0, b)
        a_pieces(1)
    for s in (P0, AM, AP, A2):
        convert(0, s)
        a_pieces(1)
    start(1)
    for b in range(NB):
        stage2b(0, b)
        a_pieces(1)
    more(1)
    a_pieces(T // APIECE)
    for s in (BM, BP):
        convert(0, s)
    for b in range(NB):
        stage3(0, b)
    convert(0, B2)
    for copy in table_copies():
        copy.wait()
    fill(1, 0)
    stage4(0)

    def both(*runs):
        def go():
            for f, *args in runs:
                f(*args)
        return go

    compute(0, {
        0: both((relay, 1, 0), (relay, 1, 2)),
        1: both((fill, 1, 2), (across, 1, 0)),
        2: both((across, 1, 1), (stage2, 1, 0), (stage2, 1, 1)),
        3: both((stage2, 1, 2), (stage2, 1, 3), (across, 1, 2), (rest, 1, 0)),
        4: both((across, 1, 3), (rest, 1, 2)),
    })
    sums_start(0)
    for s in (P0, AM, AP, A2):
        convert(1, s)
    for b in range(NB):
        stage2b(1, b)
    for b in range(NB):
        stage3(1, b)
    first_x(0)
    for s in (BM, BP):
        convert(1, s)
    convert(1, B2)
    stage4(1)

    compute(1, {
        0: both((adj_late, 0, 0)),
        1: both((adj_late, 0, 1)),
        2: both((first_add, 0)),
        3: both((own_sum, 0, 0)),
        4: both((adj_late, 0, 2)),
    })
    sums_start(1)
    adj_late(1, 0)
    own_sum(0, 1)
    first_add(1)
    adj_late(1, 1)
    own_sum(0, 2)
    final(0)
    own_sum(1, 0)
    adj_late(1, 2)
    own_sum(1, 1)
    own_sum(1, 2)
    final(1)
    for h in range(2):
        sent(recv.at[0, pl.ds(0, 15)], s_send.at[h])
        sent(recv.at[0, pl.ds(0, 7)], s_send.at[2 + h])


def shards(features, weight, adjacency_tiles, tile_rows, tile_cols, tile_counts, cluster_order):
    c = lax.axis_index("rep")
    y, xl = c // 2, c % 2
    j = jnp.arange(384, dtype=jnp.int32)
    tile_rows, tile_cols = (jnp.pad(v, (0, 384 - T)) for v in (tile_rows, tile_cols))
    dy, rx_, t = (tile_rows // 16 - y) % 4, (tile_rows // 8) % 2, tile_rows % 8
    yo = jnp.where(dy == 0, 3, jnp.where(dy == 1, 1, jnp.where(dy == 2, 0, 2)))
    rel = ((yo * 2 + (rx_ == xl)) * 4 + t % 4) * 2 + t // 4
    key = jnp.where(j < tile_counts[0], rel, 64)
    k, o = tile_cols // 8, tile_cols % 8
    panel = ((k % 2) * 8 + k // 2) * 4 + o % 4
    code = (key * 65536 + (o // 4) * 32768 + panel * 512 + j).reshape(3, 128)
    smem = pl.BlockSpec(memory_space=pltpu.SMEM)
    vmem = pl.BlockSpec(memory_space=pltpu.VMEM)
    dma = pltpu.SemaphoreType.DMA
    return pl.pallas_call(
        body,
        out_shape=jax.ShapeDtypeStruct((1024, 128), F32),
        in_specs=[smem, vmem, vmem, vmem, pl.BlockSpec(memory_space=pl.ANY)],
        out_specs=vmem,
        scratch_shapes=[
            pltpu.VMEM((2, 16, 512, 128), F32),
            pltpu.VMEM((2, 64, 128, 256), BF16),
            pltpu.VMEM((T, 128, 256), BF16),
            pltpu.VMEM((ASTAGE, APIECE, 128, 128), F32),
            pltpu.VMEM((T // 2, 128, 128), F32),
            pltpu.VMEM((2, 4, 2, 512, 128), F32),
            pltpu.VMEM((2, 4, 512 - FY, 128), F32),
            pltpu.VMEM((2, 2, 3, FY // 2, 128), F32),
            pltpu.VMEM((2, 2, 2, 512, 128), F32),
            pltpu.VMEM((2, 512, 128), F32),
            pltpu.VMEM((1024, 128), F32),
            pltpu.VMEM((2, 2, 128, 256), BF16),
            pltpu.VMEM((16, 128), jnp.int32),
            pltpu.VMEM((16, 128), F32),
            pltpu.SMEM((16, 128), jnp.int32),
            pltpu.SMEM((16, 128), F32),
            dma((2, 8, NB)),
            dma((2, 8)),
            dma((4,)),
            dma((2,)),
            dma((2, 2, 3)),
            dma((2, 2, 3, 2)),
            dma((2, 2)),
            dma((ASTAGE,)),
            dma((2,)),
        ],
        compiler_params=pltpu.CompilerParams(
            collective_id=0, has_side_effects=True, vmem_limit_bytes=63 * 1024 * 1024),
    )(cluster_order, code, features, weight, adjacency_tiles)


def solution(mesh):
    placed = (
        P(("row", "rep"), None),
        P(),
        P(("row", "rep"), None, None),
        P(("row", "rep")),
        P(("row", "rep")),
        P(("row", "rep")),
        P(("row", "rep"), None),
    )
    return jax.shard_map(
        shards, mesh=mesh, in_specs=placed, out_specs=P(("row", "rep"), None), check_vma=False
    )
```
